128 devices in a mesh: row: 8 (over y, core), col: 16 (over z, x).
Axes of the slice: x: 4, y: 4, z: 4, core: 2. Of those that a mesh axis runs over, the one named last changes fastest.
Arguments:
- front: float32 [12288, 12288], P('row', 'col'), may hold values from -6 to 6
- delayed: float32 [128, 12288], P('col', 'row'), may hold values from -6 to 6
- dest: int32 [128], P('col'), may hold values from 0 to 1023, as said below
- pivots: int32 [1024], replicated, may hold values from 0 to 12287, as said below
- pair_flags: int32 [1024], replicated, may hold values from 0 to 1, as said below
- linv: float32 [4, 256, 256], replicated, as said below
- dinv_diag: float32 [1024], replicated, may hold values from -0.1 to 0.1
- dinv_off: float32 [1024], replicated, may hold values from -0.08 to 0.08
Outputs:
- trailing: float32 [12288, 12288], P('row', 'col')
- factor: float32 [12288, 1024], P('row')
The draws below stay inside these ranges and needn't reach their ends.
Inputs may be any that keep to these rules, and one draw needn't show every extreme that they name: Distinct front columns; slots p * 256 to (p + 1) * 256 - 1 are panel p's pivots. Each block of 768 columns held by one index of col contains exactly 64 of them. `pair_flags`: A 1 at slot s joins slots s and s + 1 into one 2x2 block; no two 1s are adjacent and the last slot of a panel holds 0. `dest`: several delayed columns may share a slot. Of the 8 delayed columns held by one index of col, at most 2 go to pivot columns held by the same index of col. `linv`: each panel's matrix is unit lower triangular: ones on the diagonal, zeros above it.
All inputs are finite; a program needn't handle non-finite values.
Results may differ from the reference program's by a relative error of at most 0.00015.
Values sent between devices are 32-bit elements; how exact they have to be, the bound alone decides.
No kernel may reach another device: no remote copies, remote signals or barrier semaphores. Data moves between devices by JAX's collectives and lax.ppermute only.
A program may use at most 128 MiB of HBM per device.

```python
import jax
import jax.numpy as jnp
from jax import lax

NF = 12288
PANEL = 256
PANELS = 4
DEL_COL = 8
CAP = 2
CB = 768
E = 1024
PIV_OWN = 64
NDEL = 128
N_COL = 16


def pivot_layout(key):
    base = jax.random.fold_in(key, 7)
    picks = jax.vmap(lambda owner: jax.random.permutation(jax.random.fold_in(base, owner), CB)[:PIV_OWN].astype(jnp.int32) + owner * CB)(jnp.arange(N_COL, dtype=jnp.int32))
    listed = picks.reshape(-1).astype(jnp.int32)
    order = jax.random.permutation(jax.random.fold_in(key, 11), E).astype(jnp.int32)
    placed = jnp.zeros((E,), jnp.int32).at[order].set(listed)
    return (placed, order.reshape(N_COL, PIV_OWN))


def draw_pivots(key, part):
    return pivot_layout(key)[0]


def draw_dest(key, part):
    placed, slot_table = pivot_layout(key)
    inner = jax.random.fold_in(key, 23)
    heavy = jax.random.randint(jax.random.fold_in(inner, 1), (), 0, N_COL).astype(jnp.int32)
    shifts = jax.random.randint(jax.random.fold_in(inner, 2), (N_COL,), 0, N_COL - 1).astype(jnp.int32)
    position = jnp.arange(DEL_COL, dtype=jnp.int32)
    others = (heavy + 1 + (shifts[:, None] + position[None, :] - CAP) % (N_COL - 1)) % N_COL
    owners = jnp.where(position[None, :] < CAP, heavy, others)
    choose = jax.random.randint(jax.random.fold_in(inner, 3), (N_COL, DEL_COL), 0, PIV_OWN).astype(jnp.int32)
    return slot_table[owners, choose].reshape(-1).astype(jnp.int32)


def draw_pair_flags(key, part):
    wanted = jax.random.randint(key, (E,), 0, 5) < 2
    closing = jnp.arange(E) % PANEL == PANEL - 1

    def advance(previous, inputs):
        want_here, close_here = inputs
        result = jnp.where(want_here & (previous == 0) & jnp.logical_not(close_here), 1, 0).astype(jnp.int32)
        return (result, result)
    _, flags_out = lax.scan(advance, jnp.int32(0), (wanted, closing))
    return flags_out


def draw_linv(key, part):
    values = 0.05 * jax.random.normal(key, (PANELS, PANEL, PANEL), jnp.float32)
    lower = jnp.arange(PANEL)[:, None] > jnp.arange(PANEL)[None, :]
    return jnp.where(lower[None], values, 0.0) + jnp.eye(PANEL, dtype=jnp.float32)[None]


def steps_of(rng, shape, pieces, smallest, top_value):
    def one(dim, shards_of):
        steps = jax.random.uniform(jax.random.fold_in(jax.random.fold_in(rng, 6), dim), (shards_of,), jnp.float32, smallest / len(pieces), top_value / len(pieces))
        return jnp.repeat(jnp.exp(steps), shape[dim] // shards_of).reshape((-1,) + (1,) * (len(shape) - dim - 1))

    level = one(*pieces[0])
    for cut in pieces[1:]:
        level = level * one(*cut)
    return level


def noise(key, shape, deviation, reach, cuts=(), held_as=jnp.bfloat16):
    gain = steps_of(key, shape, cuts, -0.22, 0.18) if cuts else 1.0
    values = jax.random.normal(key, shape, jnp.float32) * deviation * gain
    return jnp.minimum(jnp.maximum(values, -reach), reach).astype(held_as)


def setup_inputs(seed: int = 0) -> dict:
    streams_of = jax.random.split(jax.random.key(seed), 9)
    front = noise(streams_of[0], (NF, NF), 1.0, 6.0, ((0, 8), (1, 16)), jnp.float32)
    delayed = noise(streams_of[1], (NDEL, NF), 1.0, 6.0, ((0, 16), (1, 8)), jnp.float32)
    dest = draw_dest(jax.random.fold_in(streams_of[8], 71), 0)
    pivots = draw_pivots(jax.random.fold_in(streams_of[8], 71), 0)
    pair_flags = draw_pair_flags(jax.random.fold_in(streams_of[8], 71), 0)
    linv = draw_linv(jax.random.fold_in(streams_of[8], 71), 0)
    dinv_diag = jnp.clip(jax.random.uniform(streams_of[6], (E,), jnp.float32, -0.1, 0.1), -0.1, 0.1)
    dinv_off = jnp.clip(jax.random.uniform(streams_of[7], (E,), jnp.float32, -0.08, 0.08), -0.08, 0.08)
    return {"front": front, "delayed": delayed, "dest": dest, "pivots": pivots, "pair_flags": pair_flags, "linv": linv, "dinv_diag": dinv_diag, "dinv_off": dinv_off}


precise = lax.Precision.HIGHEST


def pair_scale(scaled, pair_bits, diag_part, off_part):
    coupled = pair_bits.astype(jnp.float32) * off_part
    zero_col = jnp.zeros_like(scaled[:, :1])
    shifted_next = jnp.concatenate([scaled[:, 1:], zero_col], axis=1)
    shifted_prev = jnp.concatenate([zero_col, scaled[:, :-1]], axis=1)
    coupled_prev = jnp.concatenate([jnp.zeros_like(coupled[:1]), coupled[:-1]])
    return scaled * diag_part + shifted_next * coupled + shifted_prev * coupled_prev


def reference(front, delayed, dest, pivots, pair_flags, linv, dinv_diag, dinv_off):
    targets = pivots[dest]
    current = front.at[:, targets].add(jnp.transpose(delayed))
    factors = []
    for panel_index in range(PANELS):
        offset = panel_index * PANEL
        chosen = pivots[offset:offset + PANEL]
        panel_cols = current[:, chosen]
        scaled = jnp.dot(panel_cols, jnp.transpose(linv[panel_index]), precision=precise)
        columns = pair_scale(scaled, pair_flags[offset:offset + PANEL], dinv_diag[offset:offset + PANEL], dinv_off[offset:offset + PANEL])
        current = current - jnp.dot(columns, jnp.transpose(scaled), precision=precise)
        factors.append(columns)
    retained = jnp.ones((NF,), jnp.float32).at[pivots].set(0.0)
    trailing = current * retained[:, None] * retained[None, :]
    return trailing, jnp.concatenate(factors, axis=1)
```

```python
import jax
import jax.numpy as jnp
from jax import lax
from jax.sharding import PartitionSpec as P

AXES = ("row", "col")
ROWS, COLS = 8, 16
OWN = 64
DEL = 8
EXT = OWN + DEL
PANEL = 256
PANELS = 4
precise = lax.Precision.HIGHEST
fine = lax.Precision.HIGH


def shift(value, y=0, core=0, z=0, x=0):
    pairs = []
    for r in range(ROWS):
        for c in range(COLS):
            to_r = (r // 2 + y) % 4 * 2 + (r % 2 + core) % 2
            to_c = (c // 4 + z) % 4 * 4 + (c % 4 + x) % 4
            pairs.append((r * COLS + c, to_r * COLS + to_c))
    return lax.ppermute(value, AXES, pairs)


def transpose_send(value, flip):
    pairs = []
    for r in range(ROWS):
        for c in range(COLS):
            block = 2 * r + ((c % 2) ^ flip)
            pairs.append((r * COLS + c, c // 2 * COLS + block))
    return lax.ppermute(value, AXES, pairs)


def ring_small(value, axis, dim):
    behind = shift(value, **{axis: 1})
    ahead = shift(value, **{axis: -1})
    across = shift(value, **{axis: 2})
    return jnp.concatenate([value, behind, across, ahead], axis=dim)


def gather_half(block, first, second):
    behind = shift(block, **{first: 1})
    ahead = shift(block, **{first: -1})
    low = jnp.concatenate([block, behind], axis=0)
    half = block.shape[1] // 2
    across = jnp.concatenate(
        [shift(behind[:, :half], **{first: 1}), shift(ahead[:, half:], **{first: -1})], axis=1
    )
    high = jnp.concatenate([across, ahead], axis=0)
    low_behind = shift(low, **{second: 1})
    low_ahead = shift(low, **{second: -1})
    high_behind = shift(high, **{second: 1})
    high_ahead = shift(high, **{second: -1})
    low_across = shift(low_behind, **{second: 1})
    high_across = shift(high_ahead, **{second: -1})
    return [(low, high), (low_behind, high_behind), (low_across, high_across), (low_ahead, high_ahead)]


def pair_scale(scaled, coupled, diag_part):
    zero_col = jnp.zeros_like(scaled[:, :1])
    shifted_next = jnp.concatenate([scaled[:, 1:], zero_col], axis=1)
    shifted_prev = jnp.concatenate([zero_col, scaled[:, :-1]], axis=1)
    coupled_prev = jnp.concatenate([jnp.zeros_like(coupled[:1]), coupled[:-1]])
    return scaled * diag_part + shifted_next * coupled + shifted_prev * coupled_prev


def dot(a, b, dims, prec=precise):
    return lax.dot_general(a, b, (dims, ((), ())), precision=prec)


def body(front, delayed, dest, pivots, pair_flags, linv, dinv_diag, dinv_off):
    rows_blk, cols_blk = front.shape
    r = lax.axis_index("row")
    c = lax.axis_index("col")
    y, core, z, x = r // 2, r % 2, c // 4, c % 4
    slots = pivots.shape[0]
    slot_ids = jnp.arange(slots, dtype=jnp.int32)
    owners = pivots // cols_blk
    before = (owners[:, None] == owners[None, :]) & (slot_ids[None, :] < slot_ids[:, None])
    position = owners * OWN + jnp.sum(before.astype(jnp.int32), axis=1)

    own_hit = position[None, :] == (c * OWN + jnp.arange(OWN, dtype=jnp.int32))[:, None]
    own_cols = jnp.sum(jnp.where(own_hit, (pivots - c * cols_blk)[None, :], 0), axis=1)
    pick = (own_cols[:, None] == jnp.arange(cols_blk, dtype=jnp.int32)[None, :]).astype(jnp.float32)
    taken = dot(pick, front, ((1,), (1,)), precise)
    piece = jnp.concatenate([taken, delayed], axis=0)

    row_hit = position[None, :] == (r * 2 * OWN + jnp.arange(2 * OWN, dtype=jnp.int32))[:, None]
    own_rows = jnp.sum(jnp.where(row_hit, (pivots - r * rows_blk)[None, :], 0), axis=1)
    pick_rows = (own_rows[:, None] == jnp.arange(rows_blk, dtype=jnp.int32)[None, :]).astype(jnp.float32)
    crossing = dot(piece, pick_rows, ((1,), (1,)), precise)
    dest_row = jnp.zeros((8, 2 * OWN), jnp.float32).at[0, :DEL].set(dest.astype(jnp.float32))
    crossing = jnp.concatenate([crossing, dest_row], axis=0)

    crossing = ring_small(ring_small(crossing, "x", 0), "z", 0)
    crossing = crossing.reshape(COLS, EXT + 8, 2 * OWN)
    dest_rel = crossing[:, EXT, :DEL].astype(jnp.int32)
    crossing = crossing[:, :EXT].reshape(COLS * EXT, 2 * OWN)
    rel = jnp.arange(COLS, dtype=jnp.int32)
    source = (z - rel // 4) % 4 * 4 + (x - rel % 4) % 4
    slot_at = jnp.sum(
        jnp.where(position[None, :] == jnp.arange(slots, dtype=jnp.int32)[:, None], slot_ids[None, :], 0), axis=1
    )
    slot_table = slot_at.reshape(COLS, OWN)
    ext_rel = jnp.concatenate([slot_table[source], dest_rel], axis=1)
    ext_abs = jnp.concatenate([slot_table, dest_rel[source]], axis=1)
    ext_rel_flat = ext_rel.reshape(-1)
    lead = slots - PANEL
    choose = (slot_ids[:lead, None] == ext_rel_flat[None, :]).astype(jnp.float32)
    block_cols = dot(choose, crossing, ((1,), (0,)), precise)
    block_cols = ring_small(block_cols, "y", 1)
    block_cols = jnp.concatenate([block_cols, shift(block_cols, core=1)], axis=1)

    rel_row = jnp.arange(ROWS, dtype=jnp.int32)
    row_source = (y - rel_row % 4) % 4 * 2 + (core + rel_row // 4) % 2
    row_slots = slot_at.reshape(ROWS, 2 * OWN)[row_source].reshape(-1)
    linv_t = jnp.transpose(linv, (0, 2, 1)).reshape(slots, PANEL)
    row_linv = jnp.take(linv_t, row_slots, axis=0)
    row_panel = row_slots // PANEL
    spread = jnp.concatenate(
        [jnp.where((row_panel == p)[:, None], row_linv, 0.0) for p in range(1, PANELS)], axis=1
    )
    cross = dot(block_cols, spread, ((1,), (0,)))

    coupled = pair_flags.astype(jnp.float32) * dinv_off
    weights = []
    weights_d = []
    tables = {}
    for p in range(PANELS):
        blocks = [None] * PANELS
        blocks[p] = jnp.transpose(linv[p])
        for q in range(p):
            total = None
            for s in range(q, p):
                term = dot(weights_d[s][q], tables[s, p], ((1,), (0,)))
                total = term if total is None else total + term
            blocks[q] = -total
        weights.append(blocks)
        lo, hi = p * PANEL, (p + 1) * PANEL
        weights_d.append(
            [None if b is None else pair_scale(b, coupled[lo:hi], dinv_diag[lo:hi]) for b in blocks]
        )
        for n in range(p + 1, PANELS):
            total = None
            for s in range(p + 1):
                part = cross[s * PANEL : (s + 1) * PANEL, (n - 1) * PANEL : n * PANEL]
                term = dot(blocks[s], part, ((0,), (0,)))
                total = term if total is None else total + term
            tables[p, n] = total
    zero = jnp.zeros((PANEL, PANEL), jnp.float32)

    def whole(parts):
        return jnp.concatenate(
            [
                jnp.concatenate([zero if parts[p][s] is None else parts[p][s] for p in range(PANELS)], axis=1)
                for s in range(PANELS)
            ],
            axis=0,
        )

    w_scaled = jnp.take(whole(weights), ext_abs.reshape(-1), axis=0)
    w_columns = jnp.take(whole(weights_d), ext_rel_flat, axis=0)

    top, bottom = piece[:, :cols_blk], piece[:, cols_blk:]
    even = c % 2 == 0
    got_a = transpose_send(jnp.where(even, top, bottom), 0)
    got_b = transpose_send(jnp.where(even, bottom, top), 1)
    strip = jnp.concatenate([jnp.where(even, got_a, got_b), jnp.where(even, got_b, got_a)], axis=0)
    col_rows = lax.all_gather(strip, "row", axis=0, tiled=True)
    col_scaled = dot(w_scaled, col_rows, ((0,), (0,)), fine)

    upper = gather_half(top, "x", "z")
    lower = gather_half(bottom, "z", "x")
    upper = jnp.concatenate([jnp.concatenate([a, b], axis=0) for a, b in upper], axis=0)
    lower = jnp.stack([jnp.concatenate([a, b], axis=0).reshape(4, EXT, cols_blk) for a, b in lower], axis=1)
    lower = lower.reshape(COLS * EXT, cols_blk)
    factor = jnp.concatenate(
        [dot(upper, w_columns, ((0,), (0,)), fine), dot(lower, w_columns, ((0,), (0,)), fine)], axis=0
    )
    row_ids = r * rows_blk + jnp.arange(rows_blk, dtype=jnp.int32)
    col_ids = c * cols_blk + jnp.arange(cols_blk, dtype=jnp.int32)
    row_in = jnp.any(row_ids[:, None] == pivots[None, :], axis=1)
    col_in = jnp.any(col_ids[:, None] == pivots[None, :], axis=1)
    trailing = front - dot(factor, col_scaled, ((1,), (0,)), fine)
    trailing = jnp.where(row_in[:, None] | col_in[None, :], 0.0, trailing)
    return (trailing, factor)


def solution(mesh):
    return jax.shard_map(
        body,
        mesh=mesh,
        in_specs=(P("row", "col"), P("col", "row"), P("col"), P(), P(), P(), P(), P()),
        out_specs=(P("row", "col"), P("row", None)),
        check_vma=False,
    )
```

```python
import jax
import jax.numpy as jnp
from jax import lax
from jax.experimental import pallas as pl
from jax.experimental.pallas import tpu as pltpu
from jax.sharding import PartitionSpec as P

AXES = ("row", "col")
ROWS, COLS = 8, 16
OWN = 64
DEL = 8
EXT = OWN + DEL
PAD = EXT + 8
PANEL = 256
PANELS = 4
SLOTS = PANEL * PANELS
LEAD = SLOTS - PANEL
KEXT = COLS * EXT
TILE = 256
F32, BF16 = jnp.float32, jnp.bfloat16
VMEM_BYTES = 56 * 1024 * 1024


def permute(value, pairs_of):
    pairs = []
    for r in range(ROWS):
        for c in range(COLS):
            to_r, to_c = pairs_of(r, c)
            pairs.append((r * COLS + c, to_r * COLS + to_c))
    return lax.ppermute(value, AXES, pairs)


def shift(value, y=0, core=0, z=0, x=0):
    return permute(
        value,
        lambda r, c: (
            (r // 2 + y) % 4 * 2 + (r % 2 + core) % 2,
            (c // 4 + z) % 4 * 4 + (c % 4 + x) % 4,
        ),
    )


def ring_small(value, axis):
    behind = shift(value, **{axis: 1})
    ahead = shift(value, **{axis: -1})
    across = shift(value, **{axis: 2})
    return jnp.concatenate([value, behind, across, ahead], axis=0)


def gather_rows(block, core):
    behind = shift(block, y=1)
    ahead = shift(block, y=-1)
    relay = jnp.where(core == 0, behind, ahead)
    across = permute(relay, lambda r, c: ((r // 2 + (1 if r % 2 == 0 else -1)) % 4 * 2 + r % 2, c))
    mine = jnp.stack([block, behind, across, ahead], axis=0)
    return mine, shift(mine, core=1)


def mm(a, b, dims=((1,), (0,))):
    return lax.dot_general(a, b, (dims, ((), ())), preferred_element_type=F32)


def split(value):
    high = value.astype(BF16)
    return high, (value - high.astype(F32)).astype(BF16)


def mm3(a, b, dims=((1,), (0,))):
    return mm(a[0], b[0], dims) + mm(a[0], b[1], dims) + mm(a[1], b[0], dims)


def pick3(value, hot):
    high = value.astype(BF16)
    rest = value - high.astype(F32)
    mid = rest.astype(BF16)
    low = (rest - mid.astype(F32)).astype(BF16)
    return mm(high, hot) + mm(mid, hot) + mm(low, hot)


def hot(cond):
    return jnp.where(cond, 1.0, 0.0).astype(BF16)


def iota(shape, dim):
    return lax.broadcasted_iota(jnp.int32, shape, dim)


def extract_kernel(cols_ref, rows_ref, dest_ref, front_ref, delayed_ref, piece_ref, crossing_ref):
    step = pl.program_id(0)
    block, width = front_ref.shape
    picked = pick3(front_ref[...], hot(iota((width, 128), 0) == cols_ref[...]))
    piece = jnp.concatenate([jnp.transpose(picked)[:OWN], delayed_ref[...]], axis=0)
    piece_ref[...] = piece
    part = pick3(piece, hot(iota((block, 2 * OWN), 0) + step * block == rows_ref[...]))

    @pl.when(step == 0)
    def _():
        crossing_ref[...] = jnp.concatenate([part, dest_ref[...]], axis=0)

    @pl.when(step > 0)
    def _():
        crossing_ref[:EXT, :] += part


def order_kernel(slots_ref, crossing_ref, out_ref):
    count = crossing_ref.shape[0]
    value = crossing_ref[...]
    high = value.astype(BF16)
    rest = value - high.astype(F32)
    mid = rest.astype(BF16)
    low = (rest - mid.astype(F32)).astype(BF16)
    for p in range(PANELS - 1):
        rows = slice(p * PANEL, (p + 1) * PANEL)
        pick = hot(iota((PANEL, count), 0) + p * PANEL == slots_ref[...])
        out_ref[rows, :] = mm(pick, high) + mm(pick, mid) + mm(pick, low)


def weight_kernel(
    row_slots_ref, mine_ref, mate_ref, linv_ref, diag_ref, next_ref, prev_ref, wh_ref, wl_ref, dh_ref, dl_ref
):
    raw = jnp.concatenate([mine_ref[i] for i in range(4)] + [mate_ref[i] for i in range(4)], axis=1)
    raw_h, raw_l = split(raw)
    linv_t = [jnp.transpose(linv_ref[p]) for p in range(PANELS)]
    linv_s = [split(v) for v in linv_t]
    cross = {}
    for p in range(1, PANELS):
        pick = hot(iota((SLOTS, PANEL), 1) + p * PANEL == row_slots_ref[...])
        rows = slice(0, p * PANEL)
        ordered = (mm(raw_h[rows], pick).astype(BF16), mm(raw_l[rows], pick).astype(BF16))
        product = mm3(ordered, linv_s[p])
        for q in range(p):
            cross[q, p] = split(product[q * PANEL : (q + 1) * PANEL])
    tables = {}
    w, wd = {}, {}
    for p in range(PANELS):
        lo = slice(p * PANEL, (p + 1) * PANEL)
        for s in range(p + 1):
            if s == p:
                value = linv_t[p]
            else:
                value = -sum(mm3(wd[s, q], tables[q, p]) for q in range(s, p))
            scaled = (
                value * diag_ref[:, lo]
                + pltpu.roll(value, PANEL - 1, 1) * next_ref[:, lo]
                + pltpu.roll(value, 1, 1) * prev_ref[:, lo]
            )
            w[s, p] = split(value)
            wd[s, p] = split(scaled)
            rows = slice(s * PANEL, (s + 1) * PANEL)
            wh_ref[rows, lo], wl_ref[rows, lo] = w[s, p]
            dh_ref[rows, lo], dl_ref[rows, lo] = wd[s, p]
        for n in range(p + 1, PANELS):
            tables[p, n] = split(sum(mm3(w[s, p], cross[s, n], ((0,), (0,))) for s in range(p + 1)))


def operand_kernel(
    pj_slots_ref, pi_slots_ref, mine_ref, mate_ref, wh_ref, wl_ref, dh_ref, dl_ref,
    bh_ref, bl_ref, ph_ref, pl_ref, sh_ref, sl_ref,
):
    width = mine_ref.shape[-1]

    def block(refs, s, p):
        rows, cols = slice(s * PANEL, (s + 1) * PANEL), slice(p * PANEL, (p + 1) * PANEL)
        return refs[0][rows, cols], refs[1][rows, cols]

    got = jnp.concatenate([mine_ref[i] for i in range(4)] + [mate_ref[i] for i in range(4)], axis=0)
    got_h, got_l = split(got)
    for p in range(PANELS):
        rows = slice(p * PANEL, (p + 1) * PANEL)
        pick = hot(iota((PANEL, KEXT), 0) + p * PANEL == pj_slots_ref[...])
        ph_ref[rows, :], pl_ref[rows, :] = split(mm(pick, got_h) + mm(pick, got_l))
    for p in range(PANELS):
        rows = slice(p * PANEL, (p + 1) * PANEL)
        total = jnp.zeros((PANEL, width), F32)
        for s in range(p + 1):
            src = slice(s * PANEL, (s + 1) * PANEL)
            total += mm3(block((wh_ref, wl_ref), s, p), (ph_ref[src, :], pl_ref[src, :]), ((0,), (0,)))
        sh_ref[rows, :], sl_ref[rows, :] = split(total)
    for s in range(PANELS):
        rows = slice(s * PANEL, (s + 1) * PANEL)
        total = jnp.zeros((PANEL, width), F32)
        for p in range(s, PANELS):
            src = slice(p * PANEL, (p + 1) * PANEL)
            total += mm3(block((dh_ref, dl_ref), s, p), (sh_ref[src, :], sl_ref[src, :]))
        ph_ref[rows, :], pl_ref[rows, :] = split(total)
    part = KEXT // 4
    for i in range(4):
        rows = slice(i * part, (i + 1) * part)
        pick = hot(iota((part, SLOTS), 1) == pi_slots_ref[rows, :])
        for p in range(PANELS):
            cols, depth = slice(p * PANEL, (p + 1) * PANEL), (p + 1) * PANEL
            bh_ref[rows, cols] = mm(pick[:, :depth], dh_ref[:depth, cols]).astype(BF16)
            bl_ref[rows, cols] = mm(pick[:, :depth], dl_ref[:depth, cols]).astype(BF16)
        bh_ref[rows, SLOTS:] = mm(pick, ph_ref[...]).astype(BF16)
        bl_ref[rows, SLOTS:] = mm(pick, pl_ref[...]).astype(BF16)


def update_kernel(piece_ref, bh_ref, bl_ref, front_ref, row_ref, col_ref, trailing_ref, factor_ref):
    value = split(piece_ref[...])
    dims = ((0,), (0,))
    factor_ref[...] = mm3(value, (bh_ref[:, :SLOTS], bl_ref[:, :SLOTS]), dims)
    change = mm3(value, (bh_ref[:, SLOTS:], bl_ref[:, SLOTS:]), dims)
    keep = (row_ref[...] > 0.0) & (col_ref[...] > 0.0)
    trailing_ref[...] = jnp.where(keep, front_ref[...] - change, 0.0)


def whole(shape):
    return pl.BlockSpec(shape, lambda i: (0,) * len(shape), pipeline_mode=pl.Buffered(1))


PARAMS = pltpu.CompilerParams(vmem_limit_bytes=VMEM_BYTES)


def body(front, delayed, dest, pivots, pair_flags, linv, dinv_diag, dinv_off):
    rows_blk, cols_blk = front.shape
    r = lax.axis_index("row")
    c = lax.axis_index("col")
    y, core, z, x = r // 2, r % 2, c // 4, c % 4
    ids = jnp.arange(SLOTS, dtype=jnp.int32)
    rank = jnp.sum((pivots[None, :] < pivots[:, None]).astype(jnp.int32), axis=1)
    placed = rank[None, :] == ids[:, None]
    sorted_pivots = jnp.sum(jnp.where(placed, pivots[None, :], 0), axis=1)
    slot_at = jnp.sum(jnp.where(placed, ids[None, :], 0), axis=1)
    own_cols = lax.dynamic_slice(sorted_pivots, (c * OWN,), (OWN,)) - c * cols_blk
    own_cols = jnp.concatenate([own_cols, jnp.full((128 - OWN,), -1, jnp.int32)])[None, :]
    own_rows = lax.dynamic_slice(sorted_pivots, (r * 2 * OWN,), (2 * OWN,))[None, :] - r * rows_blk
    dest_row = jnp.pad(dest.astype(F32)[None, :], ((0, PAD - EXT - 1), (0, 2 * OWN - DEL)))

    piece, crossing = pl.pallas_call(
        extract_kernel,
        grid=(rows_blk // TILE,),
        in_specs=[
            pl.BlockSpec((1, 128), lambda i: (0, 0)),
            pl.BlockSpec((1, 2 * OWN), lambda i: (0, 0)),
            pl.BlockSpec((PAD - EXT, 2 * OWN), lambda i: (0, 0)),
            pl.BlockSpec((TILE, cols_blk), lambda i: (i, 0)),
            pl.BlockSpec((DEL, TILE), lambda i: (0, i)),
        ],
        out_specs=[
            pl.BlockSpec((EXT, TILE), lambda i: (0, i)),
            pl.BlockSpec((PAD, 2 * OWN), lambda i: (0, 0)),
        ],
        out_shape=[
            jax.ShapeDtypeStruct((EXT, rows_blk), F32),
            jax.ShapeDtypeStruct((PAD, 2 * OWN), F32),
        ],
        compiler_params=PARAMS,
        name="extract",
    )(own_cols, own_rows, dest_row, front, delayed)

    gathered = lax.all_gather(piece, "col", axis=0, tiled=True)

    crossing = ring_small(ring_small(crossing, "x"), "z")
    dest_rel = crossing.reshape(COLS, PAD, 2 * OWN)[:, EXT, :DEL].astype(jnp.int32)
    rel = jnp.arange(COLS, dtype=jnp.int32)
    source = (z - rel // 4) % 4 * 4 + (x - rel % 4) % 4
    slot_table = slot_at.reshape(COLS, OWN)
    cross_slots = jnp.concatenate(
        [slot_table[source], dest_rel, jnp.full((COLS, PAD - EXT), -1, jnp.int32)], axis=1
    ).reshape(1, COLS * PAD)
    ext = jnp.concatenate([slot_table, dest_rel[source]], axis=1)
    ordered = pl.pallas_call(
        order_kernel,
        out_shape=jax.ShapeDtypeStruct((LEAD, 2 * OWN), F32),
        compiler_params=PARAMS,
        name="order",
    )(cross_slots, crossing)
    ordered_mine, ordered_mate = gather_rows(ordered, core)

    parity = c % 2
    sent = [
        permute(
            lax.dynamic_slice(piece, (0, (parity ^ flip) * cols_blk), (EXT, cols_blk)),
            lambda a, b, flip=flip: (b // 2, 2 * a + ((b % 2) ^ flip)),
        )
        for flip in (0, 1)
    ]
    strip_mine, strip_mate = gather_rows(jnp.concatenate(sent, axis=0), core)

    rel_row = jnp.arange(ROWS, dtype=jnp.int32)
    row_source = (y - rel_row % 4) % 4 * 2 + (core + rel_row // 4) % 2
    row_slots = slot_at.reshape(ROWS, 2 * OWN)[row_source].reshape(SLOTS, 1)
    coupled = pair_flags.astype(F32) * dinv_off
    coupled_prev = jnp.concatenate([jnp.zeros_like(coupled[:1]), coupled[:-1]])
    square = jax.ShapeDtypeStruct((SLOTS, SLOTS), BF16)
    weights = pl.pallas_call(
        weight_kernel,
        out_shape=[square] * 4,
        compiler_params=PARAMS,
        name="weights",
    )(row_slots, ordered_mine, ordered_mate, linv, dinv_diag[None, :], coupled[None, :], coupled_prev[None, :])

    pair = jnp.stack([2 * row_source + parity, 2 * row_source + 1 - parity], axis=1).reshape(COLS)
    pj_slots = ext[pair].reshape(1, KEXT)
    wide = jax.ShapeDtypeStruct((KEXT, SLOTS + cols_blk), BF16)
    scratch = pltpu.VMEM((SLOTS, cols_blk), BF16)
    operand_h, operand_l = pl.pallas_call(
        operand_kernel,
        out_shape=[wide, wide],
        scratch_shapes=[scratch] * 4,
        compiler_params=PARAMS,
        name="operand",
    )(pj_slots, ext.reshape(KEXT, 1), strip_mine, strip_mate, *weights)

    row_ids = r * rows_blk + jnp.arange(rows_blk, dtype=jnp.int32)
    col_ids = c * cols_blk + jnp.arange(cols_blk, dtype=jnp.int32)
    row_keep = 1.0 - jnp.any(row_ids[:, None] == pivots[None, :], axis=1).astype(F32)[:, None]
    col_keep = 1.0 - jnp.any(col_ids[:, None] == pivots[None, :], axis=1).astype(F32)[None, :]
    trailing, factor = pl.pallas_call(
        update_kernel,
        grid=(rows_blk // TILE,),
        in_specs=[
            pl.BlockSpec((KEXT, TILE), lambda i: (0, i)),
            whole((KEXT, SLOTS + cols_blk)),
            whole((KEXT, SLOTS + cols_blk)),
            pl.BlockSpec((TILE, cols_blk), lambda i: (i, 0)),
            pl.BlockSpec((TILE, 1), lambda i: (i, 0)),
            whole((1, cols_blk)),
        ],
        out_specs=[
            pl.BlockSpec((TILE, cols_blk), lambda i: (i, 0)),
            pl.BlockSpec((TILE, SLOTS), lambda i: (i, 0)),
        ],
        out_shape=[
            jax.ShapeDtypeStruct((rows_blk, cols_blk), F32),
            jax.ShapeDtypeStruct((rows_blk, SLOTS), F32),
        ],
        compiler_params=PARAMS,
        name="update",
    )(gathered, operand_h, operand_l, front, row_keep, col_keep)
    return (trailing, factor)


def solution(mesh):
    return jax.shard_map(
        body,
        mesh=mesh,
        in_specs=(P("row", "col"), P("col", "row"), P("col"), P(), P(), P(), P(), P()),
        out_specs=(P("row", "col"), P("row", None)),
        check_vma=False,
    )
```

```python
import jax
import jax.numpy as jnp
from jax import lax
from jax.experimental import pallas as pl
from jax.experimental.pallas import tpu as pltpu
from jax.sharding import PartitionSpec as P

AXES = ("row", "col")
ROWS, COLS = 8, 16
OWN = 64
DEL = 8
EXT = OWN + DEL
PAD = EXT + 8
PANEL = 256
PANELS = 4
SLOTS = PANEL * PANELS
LEAD = SLOTS - PANEL
KEXT = COLS * EXT
TILE = 256
F32, BF16 = jnp.float32, jnp.bfloat16
VMEM_BYTES = 56 * 1024 * 1024


def permute(value, pairs_of):
    pairs = []
    for r in range(ROWS):
        for c in range(COLS):
            to_r, to_c = pairs_of(r, c)
            pairs.append((r * COLS + c, to_r * COLS + to_c))
    return lax.ppermute(value, AXES, pairs)


def shift(value, y=0, core=0, z=0, x=0):
    return permute(
        value,
        lambda r, c: (
            (r // 2 + y) % 4 * 2 + (r % 2 + core) % 2,
            (c // 4 + z) % 4 * 4 + (c % 4 + x) % 4,
        ),
    )


def ring_small(value, axis):
    behind = shift(value, **{axis: 1})
    ahead = shift(value, **{axis: -1})
    across = shift(value, **{axis: 2})
    return jnp.concatenate([value, behind, across, ahead], axis=0)


def near_y(block):
    return shift(block, y=1), shift(block, y=-1)


def all_y(block, behind, ahead, core):
    relay = jnp.where(core == 0, behind, ahead)
    across = permute(relay, lambda r, c: ((r // 2 + (1 if r % 2 == 0 else -1)) % 4 * 2 + r % 2, c))
    return jnp.stack([block, behind, across, ahead], axis=0)


def mm(a, b, dims=((1,), (0,))):
    return lax.dot_general(a, b, (dims, ((), ())), preferred_element_type=F32)


def split(value):
    high = value.astype(BF16)
    return high, (value - high.astype(F32)).astype(BF16)


def mm3(a, b, dims=((1,), (0,))):
    return mm(a[0], b[0], dims) + mm(a[0], b[1], dims) + mm(a[1], b[0], dims)


def pick2(value, hot):
    high, low = split(value)
    return mm(high, hot) + mm(low, hot)


def hot(cond):
    return jnp.where(cond, 1.0, 0.0).astype(BF16)


def iota(shape, dim):
    return lax.broadcasted_iota(jnp.int32, shape, dim)


def extract_kernel(
    pivots_ref, dest_ref, delayed_ref, front_ref,
    piece_ref, crossing_ref, same_ref, other_ref, sorted_ref, slot_ref,
    front_buf, sems,
):
    rows_blk, width = front_buf.shape
    steps = rows_blk // TILE
    copies = []
    for i in range(steps):
        rows = pl.ds(i * TILE, TILE)
        copies.append(pltpu.make_async_copy(front_ref.at[rows, :], front_buf.at[rows, :], sems.at[i]))
        copies[-1].start()
    r, c = lax.axis_index("row"), lax.axis_index("col")

    value = pivots_ref[...].astype(F32)
    column = jnp.transpose(value)
    ranks = []
    for g in range(8):
        count = jnp.zeros((128, 128), F32)
        for h in range(8):
            count += jnp.where(value[h : h + 1, :] < column[:, g : g + 1], 1.0, 0.0)
        ranks.append(jnp.sum(count, axis=1, keepdims=True))
    lane = iota((128, 128), 1).astype(F32)
    sub = iota((128, 128), 0).astype(F32)
    for h in range(8):
        found = jnp.zeros((128, 128), F32)
        slot = jnp.zeros((128, 128), F32)
        for g in range(8):
            hit = ranks[g] == lane + 128.0 * h
            found += jnp.where(hit, column[:, g : g + 1], 0.0)
            slot += jnp.where(hit, sub + 128.0 * g, 0.0)
        sorted_ref[h : h + 1, :] = jnp.sum(found, axis=0, keepdims=True).astype(jnp.int32)
        slot_ref[h : h + 1, :] = jnp.sum(slot, axis=0, keepdims=True).astype(jnp.int32)

    own_cols = sorted_ref[pl.ds(c // 2, 1), :] - c * width
    own_rows = sorted_ref[pl.ds(r, 1), :] - r * rows_blk
    pick = hot(iota((width, 128), 0) == own_cols)
    total = jnp.zeros((EXT, 128), F32)
    for i in range(steps):
        copies[i].wait()
        rows = slice(i * TILE, (i + 1) * TILE)
        picked = jnp.transpose(pick2(front_buf[rows, :], pick))
        piece = jnp.concatenate([picked[:OWN] + picked[OWN:], delayed_ref[:, rows]], axis=0)
        piece_ref[:, rows] = piece
        total += pick2(piece, hot(iota((TILE, 128), 0) + i * TILE == own_rows))
    crossing_ref[:EXT, :] = total
    crossing_ref[EXT:, :] = jnp.zeros((PAD - EXT, 128), F32)
    crossing_ref[EXT : EXT + 1, :DEL] = dest_ref[...].astype(F32)

    @pl.when(c % 2 == 0)
    def _():
        same_ref[...] = piece_ref[:, :width]
        other_ref[...] = piece_ref[:, width:]

    @pl.when(c % 2 == 1)
    def _():
        same_ref[...] = piece_ref[:, width:]
        other_ref[...] = piece_ref[:, :width]


def order_kernel(slots_ref, crossing_ref, out_ref):
    count = crossing_ref.shape[0]
    high, low = split(crossing_ref[...])
    for p in range(PANELS - 1):
        rows = slice(p * PANEL, (p + 1) * PANEL)
        pick = hot(iota((PANEL, count), 0) + p * PANEL == slots_ref[...])
        out_ref[rows, :] = mm(pick, high) + mm(pick, low)


def weight_kernel(
    row_slots_ref, pi_slots_ref, mine_ref, mate_ref, linv_ref, diag_ref, next_ref, prev_ref,
    wh_ref, wl_ref, wide_ref,
    dh_ref, dl_ref,
):
    raw = jnp.concatenate([mine_ref[i] for i in range(4)] + [mate_ref[i] for i in range(4)], axis=1)
    raw_h, raw_l = split(raw)
    linv_t = [jnp.transpose(linv_ref[p]) for p in range(PANELS)]
    linv_s = [split(v) for v in linv_t]
    turned = jnp.transpose(row_slots_ref[...].astype(F32))
    row_slots = jnp.concatenate([turned[:, j : j + 1] for j in range(ROWS)], axis=0)
    turned = jnp.transpose(pi_slots_ref[...].astype(F32))
    pi_slots = jnp.concatenate([turned[:, j : j + 1] for j in range(COLS)], axis=0)
    cross = {}
    for p in range(1, PANELS):
        pick = hot(iota((SLOTS, PANEL), 1).astype(F32) + float(p * PANEL) == row_slots)
        rows = slice(0, p * PANEL)
        ordered = (mm(raw_h[rows], pick).astype(BF16), mm(raw_l[rows], pick).astype(BF16))
        product = mm3(ordered, linv_s[p])
        for q in range(p):
            cross[q, p] = split(product[q * PANEL : (q + 1) * PANEL])
    tables = {}
    w, wd = {}, {}
    for p in range(PANELS):
        lo = slice(p * PANEL, (p + 1) * PANEL)
        for s in range(p + 1):
            if s == p:
                value = linv_t[p]
            else:
                value = -sum(mm3(wd[s, q], tables[q, p]) for q in range(s, p))
            scaled = (
                value * diag_ref[:, lo]
                + pltpu.roll(value, PANEL - 1, 1) * next_ref[:, lo]
                + pltpu.roll(value, 1, 1) * prev_ref[:, lo]
            )
            w[s, p] = split(value)
            wd[s, p] = split(scaled)
            rows = slice(s * PANEL, (s + 1) * PANEL)
            wh_ref[rows, lo], wl_ref[rows, lo] = w[s, p]
            dh_ref[rows, lo], dl_ref[rows, lo] = wd[s, p]
        for n in range(p + 1, PANELS):
            tables[p, n] = split(sum(mm3(w[s, p], cross[s, n], ((0,), (0,))) for s in range(p + 1)))
    part = KEXT // 4
    for i in range(4):
        rows = slice(i * part, (i + 1) * part)
        low_rows = slice(KEXT + i * part, KEXT + (i + 1) * part)
        pick = hot(iota((part, SLOTS), 1).astype(F32) == pi_slots[rows])
        for p in range(PANELS):
            cols, depth = slice(p * PANEL, (p + 1) * PANEL), (p + 1) * PANEL
            wide_ref[rows, cols] = mm(pick[:, :depth], dh_ref[:depth, cols]).astype(BF16)
            wide_ref[low_rows, cols] = mm(pick[:, :depth], dl_ref[:depth, cols]).astype(BF16)


def scale_kernel(slots_ref, mine_ref, mate_ref, wh_ref, wl_ref, out_ref, ph_ref, pl_ref):
    got = jnp.concatenate([mine_ref[i] for i in range(4)] + [mate_ref[i] for i in range(4)], axis=0)
    got_h, got_l = split(got)
    for p in range(PANELS):
        rows = slice(p * PANEL, (p + 1) * PANEL)
        pick = hot(iota((PANEL, KEXT), 0) + p * PANEL == slots_ref[...])
        ph_ref[rows, :], pl_ref[rows, :] = split(mm(pick, got_h) + mm(pick, got_l))
    for p in range(PANELS):
        rows = slice(p * PANEL, (p + 1) * PANEL)
        deep = slice(0, (p + 1) * PANEL)
        total = mm3(
            (wh_ref[deep, rows], wl_ref[deep, rows]), (ph_ref[deep, :], pl_ref[deep, :]), ((0,), (0,))
        )
        out_ref[rows, :], out_ref[SLOTS + p * PANEL : SLOTS + (p + 1) * PANEL, :] = split(total)


def update_kernel(piece_ref, wide_ref, scaled_ref, front_ref, row_ref, col_ref, trailing_ref, factor_ref):
    high, low = split(piece_ref[...])
    high, low = jnp.transpose(high), jnp.transpose(low)
    factor = mm(jnp.concatenate([high, high], axis=1), wide_ref[...]) + mm(low, wide_ref[:KEXT, :])
    factor_ref[...] = factor
    high, low = split(factor)
    change = mm(jnp.concatenate([high, high], axis=1), scaled_ref[...]) + mm(low, scaled_ref[:SLOTS, :])
    keep = (row_ref[...] > 0.0) & (col_ref[...] > 0.0)
    trailing_ref[...] = jnp.where(keep, front_ref[...] - change, 0.0)


def whole(shape):
    return pl.BlockSpec(shape, lambda i: (0,) * len(shape), pipeline_mode=pl.Buffered(1))


PARAMS = pltpu.CompilerParams(vmem_limit_bytes=VMEM_BYTES)
VM = pl.BlockSpec(memory_space=pltpu.VMEM)
ANY = pl.BlockSpec(memory_space=pl.ANY)


def body(front, delayed, dest, pivots, pair_flags, linv, dinv_diag, dinv_off):
    rows_blk, cols_blk = front.shape
    r = lax.axis_index("row")
    c = lax.axis_index("col")
    y, core, z, x = r // 2, r % 2, c // 4, c % 4

    half = jax.ShapeDtypeStruct((EXT, cols_blk), F32)
    table = jax.ShapeDtypeStruct((8, 128), jnp.int32)
    piece, crossing, same, other, _, slot_at = pl.pallas_call(
        extract_kernel,
        in_specs=[VM, VM, VM, ANY],
        out_specs=[VM] * 6,
        out_shape=[
            jax.ShapeDtypeStruct((EXT, rows_blk), F32),
            jax.ShapeDtypeStruct((PAD, 2 * OWN), F32),
            half, half, table, table,
        ],
        scratch_shapes=[
            pltpu.VMEM((rows_blk, cols_blk), F32),
            pltpu.SemaphoreType.DMA((rows_blk // TILE,)),
        ],
        compiler_params=PARAMS,
        name="extract",
    )(pivots.reshape(8, 128), dest[None, :], delayed, front)

    crossing = ring_small(ring_small(crossing, "x"), "z")
    crossing, piece, same, other = lax.optimization_barrier((crossing, piece, same, other))

    gathered = lax.all_gather(piece, "col", axis=0, tiled=True)

    dest_rel = crossing.reshape(COLS, PAD, 2 * OWN)[:, EXT, :DEL].astype(jnp.int32)
    rel = jnp.arange(COLS, dtype=jnp.int32)
    source = (z - rel // 4) % 4 * 4 + (x - rel % 4) % 4
    slot_table = slot_at.reshape(COLS, OWN)
    cross_slots = jnp.concatenate(
        [slot_table[source], dest_rel, jnp.full((COLS, PAD - EXT), -1, jnp.int32)], axis=1
    ).reshape(1, COLS * PAD)
    ext = jnp.concatenate([slot_table, dest_rel[source]], axis=1)
    ordered = pl.pallas_call(
        order_kernel,
        out_shape=jax.ShapeDtypeStruct((LEAD, 2 * OWN), F32),
        compiler_params=PARAMS,
        name="order",
    )(cross_slots, crossing)
    near = near_y(ordered)

    parity = c % 2
    sent = [
        permute(
            value,
            lambda a, b, flip=flip: (
                (b // 4 + a // 2) % 4 * 2 + b % 4 // 2,
                2 * a + ((b % 2) ^ flip),
            ),
        )
        for flip, value in enumerate((same, other))
    ]

    rel_row = jnp.arange(ROWS, dtype=jnp.int32)
    row_source = (y - rel_row % 4) % 4 * 2 + (core + rel_row // 4) % 2
    row_slots = slot_at[row_source]
    coupled = pair_flags.astype(F32) * dinv_off
    coupled_prev = jnp.concatenate([jnp.zeros_like(coupled[:1]), coupled[:-1]])
    first = (row_source // 2 - z) % 4 * 4 + row_source % 2 * 2
    pair = jnp.stack([first + parity, first + 1 - parity], axis=1).reshape(COLS)
    pair_slots = ext[pair].reshape(1, KEXT)
    row_ids = r * rows_blk + jnp.arange(rows_blk, dtype=jnp.int32)
    col_ids = c * cols_blk + jnp.arange(cols_blk, dtype=jnp.int32)
    row_keep = 1.0 - jnp.any(row_ids[:, None] == pivots[None, :], axis=1).astype(F32)[:, None]
    col_keep = 1.0 - jnp.any(col_ids[:, None] == pivots[None, :], axis=1).astype(F32)[None, :]
    small = (row_slots, ext, pair_slots, row_keep, col_keep, coupled, coupled_prev)
    near, small = lax.optimization_barrier((near, small))
    row_slots, ext, pair_slots, row_keep, col_keep, coupled, coupled_prev = small

    ordered_mine = all_y(ordered, *near, core)
    strip = jnp.concatenate(sent, axis=0)
    ordered_mine, strip = lax.optimization_barrier((ordered_mine, strip))
    ordered_mate = shift(ordered_mine, core=1)
    near = near_y(strip)
    square = jax.ShapeDtypeStruct((SLOTS, SLOTS), BF16)
    weights = pl.pallas_call(
        weight_kernel,
        out_shape=[square, square, jax.ShapeDtypeStruct((2 * KEXT, SLOTS), BF16)],
        scratch_shapes=[pltpu.VMEM((SLOTS, SLOTS), BF16)] * 2,
        compiler_params=PARAMS,
        name="weights",
    )(
        row_slots, ext, ordered_mine, ordered_mate, linv,
        dinv_diag[None, :], coupled[None, :], coupled_prev[None, :],
    )
    near, (w_high, w_low, wide) = lax.optimization_barrier((near, weights))
    strip_mine = all_y(strip, *near, core)
    strip_mate = shift(strip_mine, core=1)
    scaled = pl.pallas_call(
        scale_kernel,
        out_shape=jax.ShapeDtypeStruct((2 * SLOTS, cols_blk), BF16),
        scratch_shapes=[pltpu.VMEM((SLOTS, cols_blk), BF16)] * 2,
        compiler_params=PARAMS,
        name="scale",
    )(pair_slots, strip_mine, strip_mate, w_high, w_low)

    tile = 2 * TILE
    trailing, factor = pl.pallas_call(
        update_kernel,
        grid=(rows_blk // tile,),
        in_specs=[
            pl.BlockSpec((KEXT, tile), lambda i: (0, i)),
            whole((2 * KEXT, SLOTS)),
            whole((2 * SLOTS, cols_blk)),
            pl.BlockSpec((tile, cols_blk), lambda i: (i, 0)),
            pl.BlockSpec((tile, 1), lambda i: (i, 0)),
            whole((1, cols_blk)),
        ],
        out_specs=[
            pl.BlockSpec((tile, cols_blk), lambda i: (i, 0)),
            pl.BlockSpec((tile, SLOTS), lambda i: (i, 0)),
        ],
        out_shape=[
            jax.ShapeDtypeStruct((rows_blk, cols_blk), F32),
            jax.ShapeDtypeStruct((rows_blk, SLOTS), F32),
        ],
        compiler_params=PARAMS,
        name="update",
    )(gathered, wide, scaled, front, row_keep, col_keep)
    return (trailing, factor)


def solution(mesh):
    return jax.shard_map(
        body,
        mesh=mesh,
        in_specs=(P("row", "col"), P("col", "row"), P("col"), P(), P(), P(), P(), P()),
        out_specs=(P("row", "col"), P("row", None)),
        check_vma=False,
    )
```

```python
import jax
import jax.numpy as jnp
from jax import lax
from jax.experimental import pallas as pl
from jax.experimental.pallas import tpu as pltpu
from jax.sharding import PartitionSpec as P

AXES = ("row", "col")
ROWS, COLS = 8, 16
OWN = 64
DEL = 8
EXT = OWN + DEL
PAD = EXT + 8
PANEL = 256
PANELS = 4
SLOTS = PANEL * PANELS
LEAD = SLOTS - PANEL
KEXT = COLS * EXT
TILE = 256
F32, BF16 = jnp.float32, jnp.bfloat16
VMEM_BYTES = 56 * 1024 * 1024


def permute(value, pairs_of):
    pairs = []
    for r in range(ROWS):
        for c in range(COLS):
            to_r, to_c = pairs_of(r, c)
            pairs.append((r * COLS + c, to_r * COLS + to_c))
    return lax.ppermute(value, AXES, pairs)


def shift(value, y=0, core=0, z=0, x=0):
    return permute(
        value,
        lambda r, c: (
            (r // 2 + y) % 4 * 2 + (r % 2 + core) % 2,
            (c // 4 + z) % 4 * 4 + (c % 4 + x) % 4,
        ),
    )


def ring_small(value, axis):
    behind = shift(value, **{axis: 1})
    ahead = shift(value, **{axis: -1})
    across = shift(value, **{axis: 2})
    return jnp.concatenate([value, behind, across, ahead], axis=0)


def near_y(block):
    return shift(block, y=1), shift(block, y=-1)


def all_y(block, behind, ahead, core):
    relay = jnp.where(core == 0, behind, ahead)
    across = permute(relay, lambda r, c: ((r // 2 + (1 if r % 2 == 0 else -1)) % 4 * 2 + r % 2, c))
    return jnp.stack([block, behind, across, ahead], axis=0)


def mm(a, b, dims=((1,), (0,))):
    return lax.dot_general(a, b, (dims, ((), ())), preferred_element_type=F32)


def split(value):
    high = value.astype(BF16)
    return high, (value - high.astype(F32)).astype(BF16)


def mm3(a, b, dims=((1,), (0,))):
    return mm(a[0], b[0], dims) + mm(a[0], b[1], dims) + mm(a[1], b[0], dims)


def pick2(value, hot):
    high, low = split(value)
    return mm(high, hot) + mm(low, hot)


def hot(cond):
    return jnp.where(cond, 1.0, 0.0).astype(BF16)


def iota(shape, dim):
    return lax.broadcasted_iota(jnp.int32, shape, dim)


def extract_kernel(
    pivots_ref, dest_ref, delayed_ref, front_ref,
    piece_ref, crossing_ref, same_ref, other_ref, sorted_ref, slot_ref,
    front_buf, sems,
):
    rows_blk, width = front_buf.shape
    steps = rows_blk // TILE
    copies = []
    for i in range(steps):
        rows = pl.ds(i * TILE, TILE)
        copies.append(pltpu.make_async_copy(front_ref.at[rows, :], front_buf.at[rows, :], sems.at[i]))
        copies[-1].start()
    r, c = lax.axis_index("row"), lax.axis_index("col")

    value = pivots_ref[...].astype(F32)
    column = jnp.transpose(value)
    ranks = []
    for g in range(8):
        count = jnp.zeros((128, 128), F32)
        for h in range(8):
            count += jnp.where(value[h : h + 1, :] < column[:, g : g + 1], 1.0, 0.0)
        ranks.append(jnp.sum(count, axis=1, keepdims=True))
    lane = iota((128, 128), 1).astype(F32)
    sub = iota((128, 128), 0).astype(F32)
    for h in range(8):
        found = jnp.zeros((128, 128), F32)
        slot = jnp.zeros((128, 128), F32)
        for g in range(8):
            hit = ranks[g] == lane + 128.0 * h
            found += jnp.where(hit, column[:, g : g + 1], 0.0)
            slot += jnp.where(hit, sub + 128.0 * g, 0.0)
        sorted_ref[h : h + 1, :] = jnp.sum(found, axis=0, keepdims=True).astype(jnp.int32)
        slot_ref[h : h + 1, :] = jnp.sum(slot, axis=0, keepdims=True).astype(jnp.int32)

    own_cols = sorted_ref[pl.ds(c // 2, 1), :] - c * width
    own_rows = sorted_ref[pl.ds(r, 1), :] - r * rows_blk
    pick = hot(iota((width, 128), 0) == own_cols)
    total = jnp.zeros((EXT, 128), F32)
    for i in range(steps):
        copies[i].wait()
        rows = slice(i * TILE, (i + 1) * TILE)
        picked = jnp.transpose(pick2(front_buf[rows, :], pick))
        piece = jnp.concatenate([picked[:OWN] + picked[OWN:], delayed_ref[:, rows]], axis=0)
        piece_ref[:, rows] = piece
        total += pick2(piece, hot(iota((TILE, 128), 0) + i * TILE == own_rows))
    crossing_ref[:EXT, :] = total
    crossing_ref[EXT:, :] = jnp.zeros((PAD - EXT, 128), F32)
    crossing_ref[EXT : EXT + 1, :DEL] = dest_ref[...].astype(F32)

    @pl.when(c % 2 == 0)
    def _():
        same_ref[...] = piece_ref[:, :width]
        other_ref[...] = piece_ref[:, width:]

    @pl.when(c % 2 == 1)
    def _():
        same_ref[...] = piece_ref[:, width:]
        other_ref[...] = piece_ref[:, :width]


def order_kernel(slots_ref, crossing_ref, out_ref):
    count = crossing_ref.shape[0]
    high, low = split(crossing_ref[...])
    for p in range(PANELS - 1):
        rows = slice(p * PANEL, (p + 1) * PANEL)
        pick = hot(iota((PANEL, count), 0) + p * PANEL == slots_ref[...])
        out_ref[rows, :] = mm(pick, high) + mm(pick, low)


def weight_kernel(
    row_slots_ref, mine_ref, mate_ref, linv_ref, diag_ref, next_ref, prev_ref,
    wh_ref, wl_ref, dh_ref, dl_ref,
):
    raw = jnp.concatenate([mine_ref[i] for i in range(4)] + [mate_ref[i] for i in range(4)], axis=1)
    raw_h, raw_l = split(raw)
    linv_t = [jnp.transpose(linv_ref[p]) for p in range(PANELS)]
    linv_s = [split(v) for v in linv_t]
    turned = jnp.transpose(row_slots_ref[...].astype(F32))
    row_slots = jnp.concatenate([turned[:, j : j + 1] for j in range(ROWS)], axis=0)
    cross = {}
    for p in range(1, PANELS):
        pick = hot(iota((SLOTS, PANEL), 1).astype(F32) + float(p * PANEL) == row_slots)
        rows = slice(0, p * PANEL)
        ordered = (mm(raw_h[rows], pick).astype(BF16), mm(raw_l[rows], pick).astype(BF16))
        product = mm3(ordered, linv_s[p])
        for q in range(p):
            cross[q, p] = split(product[q * PANEL : (q + 1) * PANEL])
    tables = {}
    w, wd = {}, {}
    for p in range(PANELS):
        lo = slice(p * PANEL, (p + 1) * PANEL)
        for s in range(p + 1):
            if s == p:
                value = linv_t[p]
            else:
                value = -sum(mm3(wd[s, q], tables[q, p]) for q in range(s, p))
            scaled = (
                value * diag_ref[:, lo]
                + pltpu.roll(value, PANEL - 1, 1) * next_ref[:, lo]
                + pltpu.roll(value, 1, 1) * prev_ref[:, lo]
            )
            w[s, p] = split(value)
            wd[s, p] = split(scaled)
            rows = slice(s * PANEL, (s + 1) * PANEL)
            wh_ref[rows, lo], wl_ref[rows, lo] = w[s, p]
            dh_ref[rows, lo], dl_ref[rows, lo] = wd[s, p]
        for n in range(p + 1, PANELS):
            tables[p, n] = split(sum(mm3(w[s, p], cross[s, n], ((0,), (0,))) for s in range(p + 1)))


def expand_kernel(pi_slots_ref, dh_ref, dl_ref, wide_ref):
    turned = jnp.transpose(pi_slots_ref[...].astype(F32))
    pi_slots = jnp.concatenate([turned[:, j : j + 1] for j in range(COLS)], axis=0)
    part = KEXT // 4
    for i in range(4):
        rows = slice(i * part, (i + 1) * part)
        low_rows = slice(KEXT + i * part, KEXT + (i + 1) * part)
        pick = hot(iota((part, SLOTS), 1).astype(F32) == pi_slots[rows])
        for p in range(PANELS):
            cols, depth = slice(p * PANEL, (p + 1) * PANEL), (p + 1) * PANEL
            wide_ref[rows, cols] = mm(pick[:, :depth], dh_ref[:depth, cols]).astype(BF16)
            wide_ref[low_rows, cols] = mm(pick[:, :depth], dl_ref[:depth, cols]).astype(BF16)


def scale_kernel(slots_ref, mine_ref, mate_ref, wh_ref, wl_ref, out_ref, ph_ref, pl_ref):
    got = jnp.concatenate([mine_ref[i] for i in range(4)] + [mate_ref[i] for i in range(4)], axis=0)
    got_h, got_l = split(got)
    for p in range(PANELS):
        rows = slice(p * PANEL, (p + 1) * PANEL)
        pick = hot(iota((PANEL, KEXT), 0) + p * PANEL == slots_ref[...])
        ph_ref[rows, :], pl_ref[rows, :] = split(mm(pick, got_h) + mm(pick, got_l))
    for p in range(PANELS):
        rows = slice(p * PANEL, (p + 1) * PANEL)
        deep = slice(0, (p + 1) * PANEL)
        total = mm3(
            (wh_ref[deep, rows], wl_ref[deep, rows]), (ph_ref[deep, :], pl_ref[deep, :]), ((0,), (0,))
        )
        out_ref[rows, :], out_ref[SLOTS + p * PANEL : SLOTS + (p + 1) * PANEL, :] = split(total)


def update_kernel(piece_ref, wide_ref, scaled_ref, front_ref, row_ref, col_ref, trailing_ref, factor_ref):
    high, low = split(piece_ref[...])
    high, low = jnp.transpose(high), jnp.transpose(low)
    factor = mm(jnp.concatenate([high, high], axis=1), wide_ref[...]) + mm(low, wide_ref[:KEXT, :])
    factor_ref[...] = factor
    high, low = split(factor)
    change = mm(jnp.concatenate([high, high], axis=1), scaled_ref[...]) + mm(low, scaled_ref[:SLOTS, :])
    keep = (row_ref[...] > 0.0) & (col_ref[...] > 0.0)
    trailing_ref[...] = jnp.where(keep, front_ref[...] - change, 0.0)


def whole(shape):
    return pl.BlockSpec(shape, lambda i: (0,) * len(shape), pipeline_mode=pl.Buffered(1))


PARAMS = pltpu.CompilerParams(vmem_limit_bytes=VMEM_BYTES)
VM = pl.BlockSpec(memory_space=pltpu.VMEM)
ANY = pl.BlockSpec(memory_space=pl.ANY)


def body(front, delayed, dest, pivots, pair_flags, linv, dinv_diag, dinv_off):
    rows_blk, cols_blk = front.shape
    r = lax.axis_index("row")
    c = lax.axis_index("col")
    y, core, z, x = r // 2, r % 2, c // 4, c % 4

    half = jax.ShapeDtypeStruct((EXT, cols_blk), F32)
    table = jax.ShapeDtypeStruct((8, 128), jnp.int32)
    piece, crossing, same, other, _, slot_at = pl.pallas_call(
        extract_kernel,
        in_specs=[VM, VM, VM, ANY],
        out_specs=[VM] * 6,
        out_shape=[
            jax.ShapeDtypeStruct((EXT, rows_blk), F32),
            jax.ShapeDtypeStruct((PAD, 2 * OWN), F32),
            half, half, table, table,
        ],
        scratch_shapes=[
            pltpu.VMEM((rows_blk, cols_blk), F32),
            pltpu.SemaphoreType.DMA((rows_blk // TILE,)),
        ],
        compiler_params=PARAMS,
        name="extract",
    )(pivots.reshape(8, 128), dest[None, :], delayed, front)

    crossing = ring_small(ring_small(crossing, "x"), "z")
    crossing, piece, same, other = lax.optimization_barrier((crossing, piece, same, other))

    gathered = lax.all_gather(piece, "col", axis=0, tiled=True)

    dest_rel = crossing.reshape(COLS, PAD, 2 * OWN)[:, EXT, :DEL].astype(jnp.int32)
    rel = jnp.arange(COLS, dtype=jnp.int32)
    source = (z - rel // 4) % 4 * 4 + (x - rel % 4) % 4
    slot_table = slot_at.reshape(COLS, OWN)
    cross_slots = jnp.concatenate(
        [slot_table[source], dest_rel, jnp.full((COLS, PAD - EXT), -1, jnp.int32)], axis=1
    ).reshape(1, COLS * PAD)
    ext = jnp.concatenate([slot_table, dest_rel[source]], axis=1)
    ordered = pl.pallas_call(
        order_kernel,
        out_shape=jax.ShapeDtypeStruct((LEAD, 2 * OWN), F32),
        compiler_params=PARAMS,
        name="order",
    )(cross_slots, crossing)
    ordered, pivots, slot_at = lax.optimization_barrier((ordered, pivots, slot_at))
    near = near_y(ordered)

    parity = c % 2
    sent = [
        permute(
            value,
            lambda a, b, flip=flip: (
                (b // 4 + a // 2) % 4 * 2 + b % 4 // 2,
                2 * a + ((b % 2) ^ flip),
            ),
        )
        for flip, value in enumerate((same, other))
    ]

    rel_row = jnp.arange(ROWS, dtype=jnp.int32)
    row_source = (y - rel_row % 4) % 4 * 2 + (core + rel_row // 4) % 2
    row_slots = slot_at[row_source]
    coupled = pair_flags.astype(F32) * dinv_off
    coupled_prev = jnp.concatenate([jnp.zeros_like(coupled[:1]), coupled[:-1]])
    first = (row_source // 2 - z) % 4 * 4 + row_source % 2 * 2
    pair = jnp.stack([first + parity, first + 1 - parity], axis=1).reshape(COLS)
    pair_slots = ext[pair].reshape(1, KEXT)
    row_ids = r * rows_blk + jnp.arange(rows_blk, dtype=jnp.int32)
    col_ids = c * cols_blk + jnp.arange(cols_blk, dtype=jnp.int32)
    row_keep = 1.0 - jnp.any(row_ids[:, None] == pivots[None, :], axis=1).astype(F32)[:, None]
    col_keep = 1.0 - jnp.any(col_ids[:, None] == pivots[None, :], axis=1).astype(F32)[None, :]
    small = (row_slots, ext, pair_slots, row_keep, col_keep, coupled, coupled_prev)
    near, small = lax.optimization_barrier((near, small))
    row_slots, ext, pair_slots, row_keep, col_keep, coupled, coupled_prev = small

    ordered_mine = all_y(ordered, *near, core)
    strip = jnp.concatenate(sent, axis=0)
    ordered_mine, strip = lax.optimization_barrier((ordered_mine, strip))
    ordered_mate = shift(ordered_mine, core=1)
    near = near_y(strip)
    square = jax.ShapeDtypeStruct((SLOTS, SLOTS), BF16)
    weights = pl.pallas_call(
        weight_kernel,
        out_shape=[square] * 4,
        compiler_params=PARAMS,
        name="weights",
    )(
        row_slots, ordered_mine, ordered_mate, linv,
        dinv_diag[None, :], coupled[None, :], coupled_prev[None, :],
    )
    near, (w_high, w_low, wd_high, wd_low) = lax.optimization_barrier((near, weights))
    strip_mine = all_y(strip, *near, core)
    wide = pl.pallas_call(
        expand_kernel,
        out_shape=jax.ShapeDtypeStruct((2 * KEXT, SLOTS), BF16),
        compiler_params=PARAMS,
        name="expand",
    )(ext, wd_high, wd_low)
    strip_mine, wide = lax.optimization_barrier((strip_mine, wide))
    strip_mate = shift(strip_mine, core=1)
    scaled = pl.pallas_call(
        scale_kernel,
        out_shape=jax.ShapeDtypeStruct((2 * SLOTS, cols_blk), BF16),
        scratch_shapes=[pltpu.VMEM((SLOTS, cols_blk), BF16)] * 2,
        compiler_params=PARAMS,
        name="scale",
    )(pair_slots, strip_mine, strip_mate, w_high, w_low)

    tile = 2 * TILE
    trailing, factor = pl.pallas_call(
        update_kernel,
        grid=(rows_blk // tile,),
        in_specs=[
            pl.BlockSpec((KEXT, tile), lambda i: (0, i)),
            whole((2 * KEXT, SLOTS)),
            whole((2 * SLOTS, cols_blk)),
            pl.BlockSpec((tile, cols_blk), lambda i: (i, 0)),
            pl.BlockSpec((tile, 1), lambda i: (i, 0)),
            whole((1, cols_blk)),
        ],
        out_specs=[
            pl.BlockSpec((tile, cols_blk), lambda i: (i, 0)),
            pl.BlockSpec((tile, SLOTS), lambda i: (i, 0)),
        ],
        out_shape=[
            jax.ShapeDtypeStruct((rows_blk, cols_blk), F32),
            jax.ShapeDtypeStruct((rows_blk, SLOTS), F32),
        ],
        compiler_params=PARAMS,
        name="update",
    )(gathered, wide, scaled, front, row_keep, col_keep)
    return (trailing, factor)


def solution(mesh):
    return jax.shard_map(
        body,
        mesh=mesh,
        in_specs=(P("row", "col"), P("col", "row"), P("col"), P(), P(), P(), P(), P()),
        out_specs=(P("row", "col"), P("row", None)),
        check_vma=False,
    )
```

```python
import jax
import jax.numpy as jnp
from jax import lax
from jax.experimental import pallas as pl
from jax.experimental.pallas import tpu as pltpu
from jax.sharding import PartitionSpec as P

AXES = ("row", "col")
ROWS, COLS = 8, 16
OWN = 64
DEL = 8
EXT = OWN + DEL
PAD = EXT + 8
PANEL = 256
PANELS = 4
SLOTS = PANEL * PANELS
LEAD = SLOTS - PANEL
KEXT = COLS * EXT
TILE = 256
F32, BF16 = jnp.float32, jnp.bfloat16
VMEM_BYTES = 56 * 1024 * 1024


def permute(value, pairs_of):
    pairs = []
    for r in range(ROWS):
        for c in range(COLS):
            to_r, to_c = pairs_of(r, c)
            pairs.append((r * COLS + c, to_r * COLS + to_c))
    return lax.ppermute(value, AXES, pairs)


def shift(value, y=0, core=0, z=0, x=0):
    return permute(
        value,
        lambda r, c: (
            (r // 2 + y) % 4 * 2 + (r % 2 + core) % 2,
            (c // 4 + z) % 4 * 4 + (c % 4 + x) % 4,
        ),
    )


def ring_small(value, axis):
    behind = shift(value, **{axis: 1})
    ahead = shift(value, **{axis: -1})
    across = shift(value, **{axis: 2})
    return jnp.concatenate([value, behind, across, ahead], axis=0)


def near_y(block):
    return shift(block, y=1), shift(block, y=-1)


def far_y(behind, ahead, core):
    relay = jnp.where(core == 0, behind, ahead)
    return permute(relay, lambda r, c: ((r // 2 + (1 if r % 2 == 0 else -1)) % 4 * 2 + r % 2, c))


def all_y(block, behind, ahead, core):
    relay = jnp.where(core == 0, behind, ahead)
    across = permute(relay, lambda r, c: ((r // 2 + (1 if r % 2 == 0 else -1)) % 4 * 2 + r % 2, c))
    return jnp.stack([block, behind, across, ahead], axis=0)


def mm(a, b, dims=((1,), (0,))):
    return lax.dot_general(a, b, (dims, ((), ())), preferred_element_type=F32)


def split(value):
    high = value.astype(BF16)
    return high, (value - high.astype(F32)).astype(BF16)


def mm3(a, b, dims=((1,), (0,))):
    return mm(a[0], b[0], dims) + mm(a[0], b[1], dims) + mm(a[1], b[0], dims)


def pick2(value, hot):
    high, low = split(value)
    return mm(high, hot) + mm(low, hot)


def hot(cond):
    return jnp.where(cond, 1.0, 0.0).astype(BF16)


def iota(shape, dim):
    return lax.broadcasted_iota(jnp.int32, shape, dim)


def extract_kernel(
    pivots_ref, dest_ref, delayed_ref, front_ref,
    piece_ref, crossing_ref, same_ref, other_ref, sorted_ref, slot_ref,
    front_buf, sems,
):
    rows_blk, width = front_buf.shape
    steps = rows_blk // TILE
    copies = []
    for i in range(steps):
        rows = pl.ds(i * TILE, TILE)
        copies.append(pltpu.make_async_copy(front_ref.at[rows, :], front_buf.at[rows, :], sems.at[i]))
        copies[-1].start()
    r, c = lax.axis_index("row"), lax.axis_index("col")

    value = pivots_ref[...].astype(F32)
    column = jnp.transpose(value)
    ranks = []
    for g in range(8):
        count = jnp.zeros((128, 128), F32)
        for h in range(8):
            count += jnp.where(value[h : h + 1, :] < column[:, g : g + 1], 1.0, 0.0)
        ranks.append(jnp.sum(count, axis=1, keepdims=True))
    lane = iota((128, 128), 1).astype(F32)
    sub = iota((128, 128), 0).astype(F32)
    for h in range(8):
        found = jnp.zeros((128, 128), F32)
        slot = jnp.zeros((128, 128), F32)
        for g in range(8):
            hit = ranks[g] == lane + 128.0 * h
            found += jnp.where(hit, column[:, g : g + 1], 0.0)
            slot += jnp.where(hit, sub + 128.0 * g, 0.0)
        sorted_ref[h : h + 1, :] = jnp.sum(found, axis=0, keepdims=True).astype(jnp.int32)
        slot_ref[h : h + 1, :] = jnp.sum(slot, axis=0, keepdims=True).astype(jnp.int32)

    own_cols = sorted_ref[pl.ds(c // 2, 1), :] - c * width
    own_rows = sorted_ref[pl.ds(r, 1), :] - r * rows_blk
    pick = hot(iota((width, 128), 0) == own_cols)
    total = jnp.zeros((EXT, 128), F32)
    for i in range(steps):
        copies[i].wait()
        rows = slice(i * TILE, (i + 1) * TILE)
        picked = jnp.transpose(pick2(front_buf[rows, :], pick))
        piece = jnp.concatenate([picked[:OWN] + picked[OWN:], delayed_ref[:, rows]], axis=0)
        piece_ref[:, rows] = piece
        total += pick2(piece, hot(iota((TILE, 128), 0) + i * TILE == own_rows))
    crossing_ref[:EXT, :] = total
    crossing_ref[EXT:, :] = jnp.zeros((PAD - EXT, 128), F32)
    crossing_ref[EXT : EXT + 1, :DEL] = dest_ref[...].astype(F32)

    @pl.when(c % 2 == 0)
    def _():
        same_ref[...] = piece_ref[:, :width]
        other_ref[...] = piece_ref[:, width:]

    @pl.when(c % 2 == 1)
    def _():
        same_ref[...] = piece_ref[:, width:]
        other_ref[...] = piece_ref[:, :width]


def order_kernel(slots_ref, crossing_ref, out_ref):
    count = crossing_ref.shape[0]
    high, low = split(crossing_ref[...])
    for p in range(PANELS - 1):
        rows = slice(p * PANEL, (p + 1) * PANEL)
        pick = hot(iota((PANEL, count), 0) + p * PANEL == slots_ref[...])
        out_ref[rows, :] = mm(pick, high) + mm(pick, low)


def weight_kernel(
    row_slots_ref, mine_ref, mate_ref, linv_ref, diag_ref, next_ref, prev_ref,
    wh_ref, wl_ref, dh_ref, dl_ref,
):
    raw = jnp.concatenate([mine_ref[i] for i in range(4)] + [mate_ref[i] for i in range(4)], axis=1)
    raw_h, raw_l = split(raw)
    linv_t = [jnp.transpose(linv_ref[p]) for p in range(PANELS)]
    linv_s = [split(v) for v in linv_t]
    turned = jnp.transpose(row_slots_ref[...].astype(F32))
    row_slots = jnp.concatenate([turned[:, j : j + 1] for j in range(ROWS)], axis=0)
    cross = {}
    for p in range(1, PANELS):
        pick = hot(iota((SLOTS, PANEL), 1).astype(F32) + float(p * PANEL) == row_slots)
        rows = slice(0, p * PANEL)
        ordered = (mm(raw_h[rows], pick).astype(BF16), mm(raw_l[rows], pick).astype(BF16))
        product = mm3(ordered, linv_s[p])
        for q in range(p):
            cross[q, p] = split(product[q * PANEL : (q + 1) * PANEL])
    tables = {}
    w, wd = {}, {}
    for p in range(PANELS):
        lo = slice(p * PANEL, (p + 1) * PANEL)
        for s in range(p + 1):
            if s == p:
                value = linv_t[p]
            else:
                value = -sum(mm3(wd[s, q], tables[q, p]) for q in range(s, p))
            scaled = (
                value * diag_ref[:, lo]
                + pltpu.roll(value, PANEL - 1, 1) * next_ref[:, lo]
                + pltpu.roll(value, 1, 1) * prev_ref[:, lo]
            )
            w[s, p] = split(value)
            wd[s, p] = split(scaled)
            rows = slice(s * PANEL, (s + 1) * PANEL)
            wh_ref[rows, lo], wl_ref[rows, lo] = w[s, p]
            dh_ref[rows, lo], dl_ref[rows, lo] = wd[s, p]
        for n in range(p + 1, PANELS):
            tables[p, n] = split(sum(mm3(w[s, p], cross[s, n], ((0,), (0,))) for s in range(p + 1)))


def expand_kernel(pi_slots_ref, dh_ref, dl_ref, wide_ref):
    turned = jnp.transpose(pi_slots_ref[...].astype(F32))
    pi_slots = jnp.concatenate([turned[:, j : j + 1] for j in range(COLS)], axis=0)
    part = KEXT // 4
    for i in range(4):
        rows = slice(i * part, (i + 1) * part)
        low_rows = slice(KEXT + i * part, KEXT + (i + 1) * part)
        pick = hot(iota((part, SLOTS), 1).astype(F32) == pi_slots[rows])
        for p in range(PANELS):
            cols, depth = slice(p * PANEL, (p + 1) * PANEL), (p + 1) * PANEL
            wide_ref[rows, cols] = mm(pick[:, :depth], dh_ref[:depth, cols]).astype(BF16)
            wide_ref[low_rows, cols] = mm(pick[:, :depth], dl_ref[:depth, cols]).astype(BF16)


def scale_kernel(
    slots_ref, mine_ref, far_ref, mate_ref, far_mate_ref, wh_ref, wl_ref, out_ref, ph_ref, pl_ref
):
    got = jnp.concatenate(
        [mine_ref[i] for i in range(3)] + [far_ref[...]] + [mate_ref[i] for i in range(3)] + [far_mate_ref[...]],
        axis=0,
    )
    got_h, got_l = split(got)
    for p in range(PANELS):
        rows = slice(p * PANEL, (p + 1) * PANEL)
        pick = hot(iota((PANEL, KEXT), 0) + p * PANEL == slots_ref[...])
        ph_ref[rows, :], pl_ref[rows, :] = split(mm(pick, got_h) + mm(pick, got_l))
    for p in range(PANELS):
        rows = slice(p * PANEL, (p + 1) * PANEL)
        deep = slice(0, (p + 1) * PANEL)
        total = mm3(
            (wh_ref[deep, rows], wl_ref[deep, rows]), (ph_ref[deep, :], pl_ref[deep, :]), ((0,), (0,))
        )
        out_ref[rows, :], out_ref[SLOTS + p * PANEL : SLOTS + (p + 1) * PANEL, :] = split(total)


def update_kernel(piece_ref, wide_ref, scaled_ref, front_ref, row_ref, col_ref, trailing_ref, factor_ref):
    high, low = split(piece_ref[...])
    high, low = jnp.transpose(high), jnp.transpose(low)
    factor = mm(jnp.concatenate([high, high], axis=1), wide_ref[...]) + mm(low, wide_ref[:KEXT, :])
    factor_ref[...] = factor
    high, low = split(factor)
    change = mm(jnp.concatenate([high, high], axis=1), scaled_ref[...]) + mm(low, scaled_ref[:SLOTS, :])
    keep = (row_ref[...] > 0.0) & (col_ref[...] > 0.0)
    trailing_ref[...] = jnp.where(keep, front_ref[...] - change, 0.0)


def whole(shape):
    return pl.BlockSpec(shape, lambda i: (0,) * len(shape), pipeline_mode=pl.Buffered(1))


PARAMS = pltpu.CompilerParams(vmem_limit_bytes=VMEM_BYTES)
VM = pl.BlockSpec(memory_space=pltpu.VMEM)
ANY = pl.BlockSpec(memory_space=pl.ANY)


def body(front, delayed, dest, pivots, pair_flags, linv, dinv_diag, dinv_off):
    rows_blk, cols_blk = front.shape
    r = lax.axis_index("row")
    c = lax.axis_index("col")
    y, core, z, x = r // 2, r % 2, c // 4, c % 4

    half = jax.ShapeDtypeStruct((EXT, cols_blk), F32)
    table = jax.ShapeDtypeStruct((8, 128), jnp.int32)
    piece, crossing, same, other, _, slot_at = pl.pallas_call(
        extract_kernel,
        in_specs=[VM, VM, VM, ANY],
        out_specs=[VM] * 6,
        out_shape=[
            jax.ShapeDtypeStruct((EXT, rows_blk), F32),
            jax.ShapeDtypeStruct((PAD, 2 * OWN), F32),
            half, half, table, table,
        ],
        scratch_shapes=[
            pltpu.VMEM((rows_blk, cols_blk), F32),
            pltpu.SemaphoreType.DMA((rows_blk // TILE,)),
        ],
        compiler_params=PARAMS,
        name="extract",
    )(pivots.reshape(8, 128), dest[None, :], delayed, front)

    crossing = ring_small(ring_small(crossing, "x"), "z")
    crossing, piece, same, other = lax.optimization_barrier((crossing, piece, same, other))

    gathered = lax.all_gather(piece, "col", axis=0, tiled=True)

    dest_rel = crossing.reshape(COLS, PAD, 2 * OWN)[:, EXT, :DEL].astype(jnp.int32)
    rel = jnp.arange(COLS, dtype=jnp.int32)
    source = (z - rel // 4) % 4 * 4 + (x - rel % 4) % 4
    slot_table = slot_at.reshape(COLS, OWN)
    cross_slots = jnp.concatenate(
        [slot_table[source], dest_rel, jnp.full((COLS, PAD - EXT), -1, jnp.int32)], axis=1
    ).reshape(1, COLS * PAD)
    ext = jnp.concatenate([slot_table, dest_rel[source]], axis=1)
    ordered = pl.pallas_call(
        order_kernel,
        out_shape=jax.ShapeDtypeStruct((LEAD, 2 * OWN), F32),
        compiler_params=PARAMS,
        name="order",
    )(cross_slots, crossing)
    ordered, pivots, slot_at = lax.optimization_barrier((ordered, pivots, slot_at))
    near = near_y(ordered)

    parity = c % 2
    sent = [
        permute(
            value,
            lambda a, b, flip=flip: (
                (b // 4 + a // 2) % 4 * 2 + b % 4 // 2,
                2 * a + ((b % 2) ^ flip),
            ),
        )
        for flip, value in enumerate((same, other))
    ]

    rel_row = jnp.arange(ROWS, dtype=jnp.int32)
    row_source = (y - rel_row % 4) % 4 * 2 + (core + rel_row // 4) % 2
    row_slots = slot_at[row_source]
    coupled = pair_flags.astype(F32) * dinv_off
    coupled_prev = jnp.concatenate([jnp.zeros_like(coupled[:1]), coupled[:-1]])
    away = jnp.where(rel_row % 4 < 2, rel_row % 4, 5 - rel_row % 4)
    strip_source = (y - away) % 4 * 2 + (core + rel_row // 4) % 2
    first = (strip_source // 2 - z) % 4 * 4 + strip_source % 2 * 2
    pair = jnp.stack([first + parity, first + 1 - parity], axis=1).reshape(COLS)
    pair_slots = ext[pair].reshape(1, KEXT)
    row_ids = r * rows_blk + jnp.arange(rows_blk, dtype=jnp.int32)
    col_ids = c * cols_blk + jnp.arange(cols_blk, dtype=jnp.int32)
    row_keep = 1.0 - jnp.any(row_ids[:, None] == pivots[None, :], axis=1).astype(F32)[:, None]
    col_keep = 1.0 - jnp.any(col_ids[:, None] == pivots[None, :], axis=1).astype(F32)[None, :]
    small = (row_slots, ext, pair_slots, row_keep, col_keep, coupled, coupled_prev)
    near, small = lax.optimization_barrier((near, small))
    row_slots, ext, pair_slots, row_keep, col_keep, coupled, coupled_prev = small

    ordered_mine = all_y(ordered, *near, core)
    strip = jnp.concatenate(sent, axis=0)
    ordered_mine, strip = lax.optimization_barrier((ordered_mine, strip))
    ordered_mate = shift(ordered_mine, core=1)
    near = near_y(strip)
    square = jax.ShapeDtypeStruct((SLOTS, SLOTS), BF16)
    weights = pl.pallas_call(
        weight_kernel,
        out_shape=[square] * 4,
        compiler_params=PARAMS,
        name="weights",
    )(
        row_slots, ordered_mine, ordered_mate, linv,
        dinv_diag[None, :], coupled[None, :], coupled_prev[None, :],
    )
    near, (w_high, w_low, wd_high, wd_low) = lax.optimization_barrier((near, weights))
    strip_mine = jnp.stack([strip, *near], axis=0)
    strip_mate = shift(strip_mine, core=1)
    strip_far = far_y(*near, core)
    wide = pl.pallas_call(
        expand_kernel,
        out_shape=jax.ShapeDtypeStruct((2 * KEXT, SLOTS), BF16),
        compiler_params=PARAMS,
        name="expand",
    )(ext, wd_high, wd_low)
    strip_far, wide = lax.optimization_barrier((strip_far, wide))
    strip_far_mate = shift(strip_far, core=1)
    scaled = pl.pallas_call(
        scale_kernel,
        out_shape=jax.ShapeDtypeStruct((2 * SLOTS, cols_blk), BF16),
        scratch_shapes=[pltpu.VMEM((SLOTS, cols_blk), BF16)] * 2,
        compiler_params=PARAMS,
        name="scale",
    )(pair_slots, strip_mine, strip_far, strip_mate, strip_far_mate, w_high, w_low)

    tile = 2 * TILE
    trailing, factor = pl.pallas_call(
        update_kernel,
        grid=(rows_blk // tile,),
        in_specs=[
            pl.BlockSpec((KEXT, tile), lambda i: (0, i)),
            whole((2 * KEXT, SLOTS)),
            whole((2 * SLOTS, cols_blk)),
            pl.BlockSpec((tile, cols_blk), lambda i: (i, 0)),
            pl.BlockSpec((tile, 1), lambda i: (i, 0)),
            whole((1, cols_blk)),
        ],
        out_specs=[
            pl.BlockSpec((tile, cols_blk), lambda i: (i, 0)),
            pl.BlockSpec((tile, SLOTS), lambda i: (i, 0)),
        ],
        out_shape=[
            jax.ShapeDtypeStruct((rows_blk, cols_blk), F32),
            jax.ShapeDtypeStruct((rows_blk, SLOTS), F32),
        ],
        compiler_params=PARAMS,
        name="update",
    )(gathered, wide, scaled, front, row_keep, col_keep)
    return (trailing, factor)


def solution(mesh):
    return jax.shard_map(
        body,
        mesh=mesh,
        in_specs=(P("row", "col"), P("col", "row"), P("col"), P(), P(), P(), P(), P()),
        out_specs=(P("row", "col"), P("row", None)),
        check_vma=False,
    )
```

```python
import jax
import jax.numpy as jnp
from jax import lax
from jax.experimental import pallas as pl
from jax.experimental.pallas import tpu as pltpu
from jax.sharding import PartitionSpec as P

AXES = ("row", "col")
ROWS, COLS = 8, 16
OWN = 64
DEL = 8
EXT = OWN + DEL
PAD = EXT + 8
PANEL = 256
PANELS = 4
SLOTS = PANEL * PANELS
LEAD = SLOTS - PANEL
KEXT = COLS * EXT
TILE = 256
F32, BF16 = jnp.float32, jnp.bfloat16
VMEM_BYTES = 56 * 1024 * 1024


def permute(value, pairs_of):
    pairs = []
    for r in range(ROWS):
        for c in range(COLS):
            to_r, to_c = pairs_of(r, c)
            pairs.append((r * COLS + c, to_r * COLS + to_c))
    return lax.ppermute(value, AXES, pairs)


def shift(value, y=0, core=0, z=0, x=0):
    return permute(
        value,
        lambda r, c: (
            (r // 2 + y) % 4 * 2 + (r % 2 + core) % 2,
            (c // 4 + z) % 4 * 4 + (c % 4 + x) % 4,
        ),
    )


def ring_small(value, axis):
    behind = shift(value, **{axis: 1})
    ahead = shift(value, **{axis: -1})
    across = shift(value, **{axis: 2})
    return jnp.concatenate([value, behind, across, ahead], axis=0)


def near_y(block):
    return shift(block, y=1), shift(block, y=-1)


def far_y(behind, ahead, core):
    relay = jnp.where(core == 0, behind, ahead)
    return permute(relay, lambda r, c: ((r // 2 + (1 if r % 2 == 0 else -1)) % 4 * 2 + r % 2, c))


def all_y(block, behind, ahead, core):
    relay = jnp.where(core == 0, behind, ahead)
    across = permute(relay, lambda r, c: ((r // 2 + (1 if r % 2 == 0 else -1)) % 4 * 2 + r % 2, c))
    return jnp.stack([block, behind, across, ahead], axis=0)


def mm(a, b, dims=((1,), (0,))):
    return lax.dot_general(a, b, (dims, ((), ())), preferred_element_type=F32)


def split(value):
    high = value.astype(BF16)
    return high, (value - high.astype(F32)).astype(BF16)


def mm3(a, b, dims=((1,), (0,))):
    return mm(a[0], b[0], dims) + mm(a[0], b[1], dims) + mm(a[1], b[0], dims)


def pick2(value, hot):
    high, low = split(value)
    return mm(high, hot) + mm(low, hot)


def hot(cond):
    return jnp.where(cond, 1.0, 0.0).astype(BF16)


def iota(shape, dim):
    return lax.broadcasted_iota(jnp.int32, shape, dim)


def extract_kernel(
    pivots_ref, dest_ref, delayed_ref, front_ref,
    piece_ref, crossing_ref, same_ref, other_ref, sorted_ref, slot_ref,
    front_buf, sems,
):
    rows_blk, width = front_buf.shape
    steps = rows_blk // TILE
    copies = []
    for i in range(steps):
        rows = pl.ds(i * TILE, TILE)
        copies.append(pltpu.make_async_copy(front_ref.at[rows, :], front_buf.at[rows, :], sems.at[i]))
        copies[-1].start()
    r, c = lax.axis_index("row"), lax.axis_index("col")

    value = pivots_ref[...].astype(F32)
    column = jnp.transpose(value)
    ranks = []
    for g in range(8):
        count = jnp.zeros((128, 128), F32)
        for h in range(8):
            count += jnp.where(value[h : h + 1, :] < column[:, g : g + 1], 1.0, 0.0)
        ranks.append(jnp.sum(count, axis=1, keepdims=True))
    lane = iota((128, 128), 1).astype(F32)
    sub = iota((128, 128), 0).astype(F32)
    for h in range(8):
        found = jnp.zeros((128, 128), F32)
        slot = jnp.zeros((128, 128), F32)
        for g in range(8):
            hit = ranks[g] == lane + 128.0 * h
            found += jnp.where(hit, column[:, g : g + 1], 0.0)
            slot += jnp.where(hit, sub + 128.0 * g, 0.0)
        sorted_ref[h : h + 1, :] = jnp.sum(found, axis=0, keepdims=True).astype(jnp.int32)
        slot_ref[h : h + 1, :] = jnp.sum(slot, axis=0, keepdims=True).astype(jnp.int32)

    own_cols = sorted_ref[pl.ds(c // 2, 1), :] - c * width
    own_rows = sorted_ref[pl.ds(r, 1), :] - r * rows_blk
    pick = hot(iota((width, 128), 0) == own_cols)
    total = jnp.zeros((EXT, 128), F32)
    for i in range(steps):
        copies[i].wait()
        rows = slice(i * TILE, (i + 1) * TILE)
        picked = jnp.transpose(pick2(front_buf[rows, :], pick))
        piece = jnp.concatenate([picked[:OWN] + picked[OWN:], delayed_ref[:, rows]], axis=0)
        piece_ref[:, rows] = piece
        total += pick2(piece, hot(iota((TILE, 128), 0) + i * TILE == own_rows))
    crossing_ref[:EXT, :] = total
    crossing_ref[EXT:, :] = jnp.zeros((PAD - EXT, 128), F32)
    crossing_ref[EXT : EXT + 1, :DEL] = dest_ref[...].astype(F32)

    @pl.when(c % 2 == 0)
    def _():
        same_ref[...] = piece_ref[:, :width]
        other_ref[...] = piece_ref[:, width:]

    @pl.when(c % 2 == 1)
    def _():
        same_ref[...] = piece_ref[:, width:]
        other_ref[...] = piece_ref[:, :width]


def order_kernel(slots_ref, crossing_ref, out_ref):
    count = crossing_ref.shape[0]
    high, low = split(crossing_ref[...])
    for p in range(PANELS - 1):
        rows = slice(p * PANEL, (p + 1) * PANEL)
        pick = hot(iota((PANEL, count), 0) + p * PANEL == slots_ref[...])
        out_ref[rows, :] = mm(pick, high) + mm(pick, low)


def weight_kernel(
    row_slots_ref, mine_ref, mate_ref, linv_ref, diag_ref, next_ref, prev_ref,
    wh_ref, wl_ref, dh_ref, dl_ref,
):
    raw = jnp.concatenate([mine_ref[i] for i in range(4)] + [mate_ref[i] for i in range(4)], axis=1)
    raw_h, raw_l = split(raw)
    linv_t = [jnp.transpose(linv_ref[p]) for p in range(PANELS)]
    linv_s = [split(v) for v in linv_t]
    turned = jnp.transpose(row_slots_ref[...].astype(F32))
    row_slots = jnp.concatenate([turned[:, j : j + 1] for j in range(ROWS)], axis=0)
    cross = {}
    for p in range(1, PANELS):
        pick = hot(iota((SLOTS, PANEL), 1).astype(F32) + float(p * PANEL) == row_slots)
        rows = slice(0, p * PANEL)
        ordered = (mm(raw_h[rows], pick).astype(BF16), mm(raw_l[rows], pick).astype(BF16))
        product = mm3(ordered, linv_s[p])
        for q in range(p):
            cross[q, p] = split(product[q * PANEL : (q + 1) * PANEL])
    tables = {}
    w, wd = {}, {}
    for p in range(PANELS):
        lo = slice(p * PANEL, (p + 1) * PANEL)
        for s in range(p + 1):
            if s == p:
                value = linv_t[p]
            else:
                value = -sum(mm3(wd[s, q], tables[q, p]) for q in range(s, p))
            scaled = (
                value * diag_ref[:, lo]
                + pltpu.roll(value, PANEL - 1, 1) * next_ref[:, lo]
                + pltpu.roll(value, 1, 1) * prev_ref[:, lo]
            )
            w[s, p] = split(value)
            wd[s, p] = split(scaled)
            rows = slice(s * PANEL, (s + 1) * PANEL)
            wh_ref[rows, lo], wl_ref[rows, lo] = w[s, p]
            dh_ref[rows, lo], dl_ref[rows, lo] = wd[s, p]
        for n in range(p + 1, PANELS):
            tables[p, n] = split(sum(mm3(w[s, p], cross[s, n], ((0,), (0,))) for s in range(p + 1)))


def expand_kernel(pi_slots_ref, dh_ref, dl_ref, wide_ref):
    turned = jnp.transpose(pi_slots_ref[...].astype(F32))
    pi_slots = jnp.concatenate([turned[:, j : j + 1] for j in range(COLS)], axis=0)
    part = KEXT // 4
    for i in range(4):
        rows = slice(i * part, (i + 1) * part)
        low_rows = slice(KEXT + i * part, KEXT + (i + 1) * part)
        pick = hot(iota((part, SLOTS), 1).astype(F32) == pi_slots[rows])
        for p in range(PANELS):
            cols, depth = slice(p * PANEL, (p + 1) * PANEL), (p + 1) * PANEL
            wide_ref[rows, cols] = mm(pick[:, :depth], dh_ref[:depth, cols]).astype(BF16)
            wide_ref[low_rows, cols] = mm(pick[:, :depth], dl_ref[:depth, cols]).astype(BF16)


def scale_kernel(
    slots_ref, mine_ref, far_ref, mate_ref, far_mate_ref, high_ref, low_ref,
    out_ref, ph_ref, pl_ref, wh_ref, wl_ref, sems,
):
    copies = [
        pltpu.make_async_copy(high_ref, wh_ref, sems.at[0]),
        pltpu.make_async_copy(low_ref, wl_ref, sems.at[1]),
    ]
    for done in copies:
        done.start()
    got = jnp.concatenate(
        [mine_ref[i] for i in range(3)] + [far_ref[...]] + [mate_ref[i] for i in range(3)] + [far_mate_ref[...]],
        axis=0,
    )
    got_h, got_l = split(got)
    for p in range(PANELS):
        rows = slice(p * PANEL, (p + 1) * PANEL)
        pick = hot(iota((PANEL, KEXT), 0) + p * PANEL == slots_ref[...])
        ph_ref[rows, :], pl_ref[rows, :] = split(mm(pick, got_h) + mm(pick, got_l))
    for done in copies:
        done.wait()
    for p in range(PANELS):
        rows = slice(p * PANEL, (p + 1) * PANEL)
        deep = slice(0, (p + 1) * PANEL)
        total = mm3(
            (wh_ref[deep, rows], wl_ref[deep, rows]), (ph_ref[deep, :], pl_ref[deep, :]), ((0,), (0,))
        )
        out_ref[rows, :], out_ref[SLOTS + p * PANEL : SLOTS + (p + 1) * PANEL, :] = split(total)


def update_kernel(piece_ref, wide_ref, scaled_ref, front_ref, row_ref, col_ref, trailing_ref, factor_ref):
    high, low = split(piece_ref[...])
    high, low = jnp.transpose(high), jnp.transpose(low)
    factor = mm(jnp.concatenate([high, high], axis=1), wide_ref[...]) + mm(low, wide_ref[:KEXT, :])
    factor_ref[...] = factor
    high, low = split(factor)
    change = mm(jnp.concatenate([high, high], axis=1), scaled_ref[...]) + mm(low, scaled_ref[:SLOTS, :])
    keep = (row_ref[...] > 0.0) & (col_ref[...] > 0.0)
    trailing_ref[...] = jnp.where(keep, front_ref[...] - change, 0.0)


def whole(shape):
    return pl.BlockSpec(shape, lambda i: (0,) * len(shape), pipeline_mode=pl.Buffered(1))


PARAMS = pltpu.CompilerParams(vmem_limit_bytes=VMEM_BYTES)
VM = pl.BlockSpec(memory_space=pltpu.VMEM)
ANY = pl.BlockSpec(memory_space=pl.ANY)


def body(front, delayed, dest, pivots, pair_flags, linv, dinv_diag, dinv_off):
    rows_blk, cols_blk = front.shape
    r = lax.axis_index("row")
    c = lax.axis_index("col")
    y, core, z, x = r // 2, r % 2, c // 4, c % 4

    half = jax.ShapeDtypeStruct((EXT, cols_blk), F32)
    table = jax.ShapeDtypeStruct((8, 128), jnp.int32)
    piece, crossing, same, other, _, slot_at = pl.pallas_call(
        extract_kernel,
        in_specs=[VM, VM, VM, ANY],
        out_specs=[VM] * 6,
        out_shape=[
            jax.ShapeDtypeStruct((EXT, rows_blk), F32),
            jax.ShapeDtypeStruct((PAD, 2 * OWN), F32),
            half, half, table, table,
        ],
        scratch_shapes=[
            pltpu.VMEM((rows_blk, cols_blk), F32),
            pltpu.SemaphoreType.DMA((rows_blk // TILE,)),
        ],
        compiler_params=PARAMS,
        name="extract",
    )(pivots.reshape(8, 128), dest[None, :], delayed, front)

    crossing = ring_small(ring_small(crossing, "x"), "z")
    crossing, piece, same, other = lax.optimization_barrier((crossing, piece, same, other))

    gathered = lax.all_gather(piece, "col", axis=0, tiled=True)

    dest_rel = crossing.reshape(COLS, PAD, 2 * OWN)[:, EXT, :DEL].astype(jnp.int32)
    rel = jnp.arange(COLS, dtype=jnp.int32)
    source = (z - rel // 4) % 4 * 4 + (x - rel % 4) % 4
    slot_table = slot_at.reshape(COLS, OWN)
    cross_slots = jnp.concatenate(
        [slot_table[source], dest_rel, jnp.full((COLS, PAD - EXT), -1, jnp.int32)], axis=1
    ).reshape(1, COLS * PAD)
    ext = jnp.concatenate([slot_table, dest_rel[source]], axis=1)
    ordered = pl.pallas_call(
        order_kernel,
        out_shape=jax.ShapeDtypeStruct((LEAD, 2 * OWN), F32),
        compiler_params=PARAMS,
        name="order",
    )(cross_slots, crossing)
    ordered, pivots, slot_at = lax.optimization_barrier((ordered, pivots, slot_at))
    near = near_y(ordered)

    parity = c % 2
    sent = [
        permute(
            value,
            lambda a, b, flip=flip: (
                (b // 4 + a // 2) % 4 * 2 + b % 4 // 2,
                2 * a + ((b % 2) ^ flip),
            ),
        )
        for flip, value in enumerate((same, other))
    ]

    rel_row = jnp.arange(ROWS, dtype=jnp.int32)
    row_source = (y - rel_row % 4) % 4 * 2 + (core + rel_row // 4) % 2
    row_slots = slot_at[row_source]
    coupled = pair_flags.astype(F32) * dinv_off
    coupled_prev = jnp.concatenate([jnp.zeros_like(coupled[:1]), coupled[:-1]])
    away = jnp.where(rel_row % 4 < 2, rel_row % 4, 5 - rel_row % 4)
    strip_source = (y - away) % 4 * 2 + (core + rel_row // 4) % 2
    first = (strip_source // 2 - z) % 4 * 4 + strip_source % 2 * 2
    pair = jnp.stack([first + parity, first + 1 - parity], axis=1).reshape(COLS)
    pair_slots = ext[pair].reshape(1, KEXT)
    row_ids = r * rows_blk + jnp.arange(rows_blk, dtype=jnp.int32)
    col_ids = c * cols_blk + jnp.arange(cols_blk, dtype=jnp.int32)
    row_keep = 1.0 - jnp.any(row_ids[:, None] == pivots[None, :], axis=1).astype(F32)[:, None]
    col_keep = 1.0 - jnp.any(col_ids[:, None] == pivots[None, :], axis=1).astype(F32)[None, :]
    small = (row_slots, ext, pair_slots, row_keep, col_keep, coupled, coupled_prev)
    near, small = lax.optimization_barrier((near, small))
    row_slots, ext, pair_slots, row_keep, col_keep, coupled, coupled_prev = small

    ordered_mine = all_y(ordered, *near, core)
    strip = jnp.concatenate(sent, axis=0)
    ordered_mine, strip = lax.optimization_barrier((ordered_mine, strip))
    ordered_mate = shift(ordered_mine, core=1)
    near = near_y(strip)
    square = jax.ShapeDtypeStruct((SLOTS, SLOTS), BF16)
    weights = pl.pallas_call(
        weight_kernel,
        out_shape=[square] * 4,
        compiler_params=PARAMS,
        name="weights",
    )(
        row_slots, ordered_mine, ordered_mate, linv,
        dinv_diag[None, :], coupled[None, :], coupled_prev[None, :],
    )
    near, (w_high, w_low, wd_high, wd_low) = lax.optimization_barrier((near, weights))
    strip_mine = jnp.stack([strip, *near], axis=0)
    strip_mate = shift(strip_mine, core=1)
    strip_far = far_y(*near, core)
    wide = pl.pallas_call(
        expand_kernel,
        out_shape=jax.ShapeDtypeStruct((2 * KEXT, SLOTS), BF16),
        compiler_params=PARAMS,
        name="expand",
    )(ext, wd_high, wd_low)
    strip_far, wide = lax.optimization_barrier((strip_far, wide))
    strip_far_mate = shift(strip_far, core=1)
    scaled = pl.pallas_call(
        scale_kernel,
        in_specs=[VM] * 5 + [ANY] * 2,
        out_specs=VM,
        out_shape=jax.ShapeDtypeStruct((2 * SLOTS, cols_blk), BF16),
        scratch_shapes=[
            pltpu.VMEM((SLOTS, cols_blk), BF16),
            pltpu.VMEM((SLOTS, cols_blk), BF16),
            pltpu.VMEM((SLOTS, SLOTS), BF16),
            pltpu.VMEM((SLOTS, SLOTS), BF16),
            pltpu.SemaphoreType.DMA((2,)),
        ],
        compiler_params=PARAMS,
        name="scale",
    )(pair_slots, strip_mine, strip_far, strip_mate, strip_far_mate, w_high, w_low)

    tile = 2 * TILE
    trailing, factor = pl.pallas_call(
        update_kernel,
        grid=(rows_blk // tile,),
        in_specs=[
            pl.BlockSpec((KEXT, tile), lambda i: (0, i)),
            whole((2 * KEXT, SLOTS)),
            whole((2 * SLOTS, cols_blk)),
            pl.BlockSpec((tile, cols_blk), lambda i: (i, 0)),
            pl.BlockSpec((tile, 1), lambda i: (i, 0)),
            whole((1, cols_blk)),
        ],
        out_specs=[
            pl.BlockSpec((tile, cols_blk), lambda i: (i, 0)),
            pl.BlockSpec((tile, SLOTS), lambda i: (i, 0)),
        ],
        out_shape=[
            jax.ShapeDtypeStruct((rows_blk, cols_blk), F32),
            jax.ShapeDtypeStruct((rows_blk, SLOTS), F32),
        ],
        compiler_params=PARAMS,
        name="update",
    )(gathered, wide, scaled, front, row_keep, col_keep)
    return (trailing, factor)


def solution(mesh):
    return jax.shard_map(
        body,
        mesh=mesh,
        in_specs=(P("row", "col"), P("col", "row"), P("col"), P(), P(), P(), P(), P()),
        out_specs=(P("row", "col"), P("row", None)),
        check_vma=False,
    )
```
